512 devices in a mesh: seq: 64 (over z_lo, y, core), tp: 8 (over z_hi, x).
Axes of the slice: x: 4, y: 8, z: 8 (z_hi: 2, z_lo: 4; z = z_hi * 4 + z_lo), core: 2. Of those that a mesh axis runs over, the one named last changes fastest.
Arguments:
- queries: bfloat16 [512, 128, 128], P('seq', 'tp'), may hold values from -92 to 92
- prefix_keys: bfloat16 [32768, 8, 128], P('seq', 'tp'), may hold values from -5 to 5
- prefix_values: bfloat16 [32768, 8, 128], P('seq', 'tp'), may hold values from -12 to 12
- suffix_keys: bfloat16 [512, 256, 8, 128], P('seq', None, 'tp'), may hold values from -8 to 8
- suffix_values: bfloat16 [512, 256, 8, 128], P('seq', None, 'tp'), may hold values from -12 to 12
- self_keys: bfloat16 [512, 8, 128], P('seq', 'tp'), may hold values from -12 to 12
- self_values: bfloat16 [512, 8, 128], P('seq', 'tp'), may hold values from -12 to 12
- suffix_lengths: int32 [512], P('seq'), may hold values from 1 to 256, as said below
- out_weight: bfloat16 [16384, 16384], P('tp', 'seq'), may hold values from -0.046875 to 0.046875
Outputs:
- mixed: bfloat16 [512, 16384], P('tp', 'seq')
The draws below stay inside these ranges and needn't reach their ends.
Inputs may be any that keep to these rules, and one draw needn't show every extreme that they name: `suffix_lengths`: at least one row has all 256 slots live and at least one has a single live slot.
All inputs are finite; a program needn't handle non-finite values.
Results may differ from the reference program's by a relative error of at most 0.025.
Values may be sent and summed in bfloat16 or wider, within the bound.
A program may use at most 128 MiB of HBM per device.

```python
import math
import jax
import jax.numpy as jnp
from jax import lax

D = 16384
H = 128
KVH = 8
HD = 128
ROW_DEV = 8
SUF = 256
ROWS = 512
PREFIX = 32768


def draw_queries(key, part):
    key = jax.random.fold_in(key, 1)
    base = jnp.clip(2.0 * jax.random.normal(key, (ROWS, H, HD), jnp.float32), -10.0, 10.0)
    return base.astype(jnp.bfloat16)


def draw_prefix_keys(key, part):
    key = jax.random.fold_in(key, 2)
    base = jnp.clip(jax.random.normal(key, (PREFIX, KVH, HD), jnp.float32), -5.0, 5.0)
    return base.astype(jnp.bfloat16)


def draw_suffix_lengths(key, part):
    key = jax.random.fold_in(key, 3)
    first_key, second_key = jax.random.split(key)
    lengths = jax.random.randint(first_key, (ROWS,), 1, SUF + 1, dtype=jnp.int32)
    picked = jax.random.permutation(second_key, ROWS)
    lengths = lengths.at[picked[0]].set(SUF)
    lengths = lengths.at[picked[1]].set(1)
    return lengths.astype(jnp.int32)


def steps_of(own_key, extent, cuts, low, largest):
    level, own = 1.0, jax.random.fold_in(own_key, 6)
    for dim, blocks in cuts:
        draws = jnp.exp(jax.random.uniform(jax.random.fold_in(own, dim), (blocks,), jnp.float32, low / len(cuts), largest / len(cuts)))
        level = level * jnp.repeat(draws, extent[dim] // blocks).reshape([-1 if axis == dim else 1 for axis in range(len(extent))])
    return level


def bell_draw(own_key, shape, spread, reach, cuts=(), kind=jnp.bfloat16):
    loudness = steps_of(own_key, shape, cuts, -0.22, 0.18) if cuts else 1.0
    result = jax.random.normal(own_key, shape, jnp.float32) * spread * loudness
    return jnp.minimum(jnp.maximum(result, -reach), reach).astype(kind)


def setup_inputs(seed: int = 0) -> dict:
    arg_keys = jax.random.split(jax.random.key(seed), 10)
    return {
        "queries": draw_queries(jax.random.fold_in(arg_keys[9], 71), 0),
        "prefix_keys": draw_prefix_keys(jax.random.fold_in(arg_keys[9], 71), 0),
        "prefix_values": bell_draw(arg_keys[2], (PREFIX, KVH, HD), 3.0, 12.0, ((0, 64), (1, 8))),
        "suffix_keys": bell_draw(arg_keys[3], (ROWS, SUF, KVH, HD), 1.5, 8.0, ((0, 64), (2, 8))),
        "suffix_values": bell_draw(arg_keys[4], (ROWS, SUF, KVH, HD), 3.0, 12.0, ((0, 64), (2, 8))),
        "self_keys": bell_draw(arg_keys[5], (ROWS, KVH, HD), 2.5, 12.0, ((0, 64), (1, 8))),
        "self_values": bell_draw(arg_keys[6], (ROWS, KVH, HD), 3.0, 12.0, ((0, 64), (1, 8))),
        "suffix_lengths": draw_suffix_lengths(jax.random.fold_in(arg_keys[9], 71), 0),
        "out_weight": bell_draw(arg_keys[8], (H * HD, D), (H * HD) ** -0.5, 0.046875, ((0, 8), (1, 64))),
    }


EPS = 1e-06

def rounded(values):
    return lax.optimization_barrier(values.astype(jnp.bfloat16)).astype(jnp.float32)

def reference(queries, prefix_keys, prefix_values, suffix_keys, suffix_values, self_keys, self_values, suffix_lengths, out_weight):
    group_size = H // KVH
    inv_root = 1.0 / math.sqrt(HD)
    blocks = ROWS // ROW_DEV
    prefix_key32 = prefix_keys.astype(jnp.float32)
    prefix_val32 = prefix_values.astype(jnp.float32)
    query_blocks = queries.reshape(blocks, ROW_DEV, KVH, group_size, HD)
    suffix_kblocks = suffix_keys.reshape(blocks, ROW_DEV, SUF, KVH, HD)
    suffix_vblocks = suffix_values.reshape(blocks, ROW_DEV, SUF, KVH, HD)
    self_kblocks = self_keys.reshape(blocks, ROW_DEV, KVH, HD)
    self_vblocks = self_values.reshape(blocks, ROW_DEV, KVH, HD)
    length_blocks = suffix_lengths.reshape(blocks, ROW_DEV)

    def one_block(block_items):
        query_b, suffix_kb, suffix_vb, self_kb, self_vb, length_b = block_items
        query_f32 = query_b.astype(jnp.float32)
        prefix_scores = jnp.einsum('rkgd,pkd->rkgp', query_f32, prefix_key32) * inv_root
        suffix_scores = jnp.einsum('rkgd,rskd->rkgs', query_f32, suffix_kb.astype(jnp.float32)) * inv_root
        self_scores = jnp.einsum('rkgd,rkd->rkg', query_f32, self_kb.astype(jnp.float32))[..., None] * inv_root
        live_mask = (jnp.arange(SUF, dtype=jnp.int32)[None, :] < length_b[:, None])[:, None, None, :]
        suffix_scores = jnp.where(live_mask, suffix_scores, 0.0)
        row_top = jnp.maximum(lax.optimization_barrier(jnp.max(prefix_scores, axis=-1)), lax.optimization_barrier(jnp.max(suffix_scores, axis=-1)))
        row_top = jnp.maximum(jnp.maximum(row_top, self_scores[..., 0]), 0.0)
        offset = jnp.exp(-row_top)[..., None]
        prefix_shift = jnp.exp(prefix_scores - row_top[..., None]) - offset
        suffix_shift = jnp.where(live_mask, jnp.exp(suffix_scores - row_top[..., None]) - offset, 0.0)
        self_shift = jnp.exp(self_scores - row_top[..., None]) - offset
        numerator = jnp.einsum('rkgp,pkd->rkgd', rounded(jnp.maximum(prefix_shift, 0.0)), prefix_val32)
        numerator = numerator + jnp.einsum('rkgs,rskd->rkgd', rounded(jnp.maximum(suffix_shift, 0.0)), suffix_vb.astype(jnp.float32))
        numerator = numerator + rounded(jnp.maximum(self_shift, 0.0)) * self_vb.astype(jnp.float32)[:, :, None, :]
        denominator = lax.optimization_barrier(jnp.sum(jnp.abs(prefix_shift), axis=-1)) + lax.optimization_barrier(jnp.sum(jnp.abs(suffix_shift), axis=-1)) + jnp.abs(self_shift[..., 0])
        attention = numerator / (denominator + EPS * jnp.exp(-row_top))[..., None]
        return attention.astype(jnp.bfloat16).reshape(ROW_DEV, H * HD)
    attention = lax.map(one_block, (query_blocks, suffix_kblocks, suffix_vblocks, self_kblocks, self_vblocks, length_blocks))
    attention = attention.reshape(ROWS, H * HD)
    return jnp.dot(attention, out_weight, preferred_element_type=jnp.float32).astype(jnp.bfloat16)
```

```python
import functools
import math

import jax
import jax.numpy as jnp
from jax import lax
from jax.experimental import pallas as pl
from jax.experimental.pallas import tpu as pltpu
from jax.sharding import PartitionSpec as P

EPS = 1e-06
MESH = pl.DeviceIdType.MESH
F32 = jnp.float32
BF16 = jnp.bfloat16

NZ, NY, NX, NZH = 4, 8, 4, 2
QROWS = 128
KEYS = 512
TILE = 256


def coordinates():
    s = lax.axis_index("seq")
    t = lax.axis_index("tp")
    return s // 16, lax.rem(s // 2, NY), lax.rem(s, 2), t // NX, lax.rem(t, NX)


def device(z, y, c, zh, x):
    return ((z * NY + y) * 2 + c, zh * NX + x)


def kernel(
    q_hbm, pk_hbm, pv_hbm, sk_hbm, sv_hbm, w_hbm, selfk_ref, selfv_ref, len_ref,
    out_ref,
    qbuf, kbuf, vbuf, skbuf, svbuf, selfk, selfv, wbuf,
    num, top, den, pn_out, ps_out, pn_in, ps_in, att, land, rows_all, prod, pieces,
    local_sem, send_sem, recv_sem,
):
    z, y, c, zh, x = coordinates()
    z_near = z + 1 - 2 * lax.rem(z, 2)
    y_near = y + 1 - 2 * lax.rem(y, 2)
    other = 1 - c
    scale = math.log2(math.e) / math.sqrt(128)

    local = [
        pltpu.make_async_copy(src, dst, local_sem.at[i])
        for i, (src, dst) in enumerate(
            [
                (q_hbm, qbuf.at[pl.ds(0, QROWS)]),
                (pk_hbm, kbuf.at[0, pl.ds(0, KEYS)]),
                (pv_hbm, vbuf.at[0, pl.ds(0, KEYS)]),
                (sk_hbm, skbuf),
                (sv_hbm, svbuf),
                (w_hbm, wbuf.at[0]),
            ]
        )
    ]
    for copy in local:
        copy.start()

    dev_core = device(z, y, other, zh, x)
    dev_ynear = device(z, y_near, c, zh, x)
    dev_znear = device(z_near, y, c, zh, x)

    def coset(r, sign):
        if sign > 0:
            zz = lax.rem(z + 2 * (r // 4), NZ)
            yy = lax.rem(y + 2 * lax.rem(r, 4), NY)
        else:
            zz = lax.rem(z + NZ - 2 * (r // 4), NZ)
            yy = lax.rem(y + NY - 2 * lax.rem(r, 4), NY)
        return device(zz, yy, c, zh, x)

    def line(r):
        return device(lax.rem(z + NZ - r, NZ), y, c, zh, x)

    dev_right = device(z, lax.rem(y + 1, NY), c, zh, x)
    dev_left = device(z, lax.rem(y + NY - 1, NY), c, zh, x)

    def owner(r):
        return device(
            z, y, lax.rem(c + lax.rem(r, 2), 2), lax.rem(zh + r // 8, NZH), lax.rem(x + lax.rem(r // 2, 4), NX)
        )

    partners = [dev_znear, dev_right, dev_left]
    partners += [coset(r, 1) for r in range(1, 8)]
    partners += [line(r) for r in range(1, NZ)]
    partners += [owner(r) for r in range(1, 16)]
    barrier = pltpu.get_barrier_semaphore()
    for partner in partners:
        pl.semaphore_signal(barrier, inc=1, device_id=partner, device_id_type=MESH)
    pl.semaphore_wait(barrier, len(partners))

    slots = iter(range(1000))

    def remote(src, dst, to, slot=None):
        slot = next(slots) if slot is None else slot
        return pltpu.make_async_remote_copy(
            src_ref=src, dst_ref=dst, send_sem=send_sem.at[slot], recv_sem=recv_sem.at[slot],
            device_id=to, device_id_type=MESH,
        )

    started = []

    def go(copy):
        copy.start()
        started.append(copy)
        return copy

    local[0].wait()
    q_copies = [
        go(remote(qbuf.at[pl.ds(0, QROWS)], qbuf.at[pl.ds(r * QROWS, QROWS)], coset(r, 1)))
        for r in range(1, 8)
    ]
    low, high = pl.ds(0, KEYS), pl.ds(KEYS, KEYS)
    local[1].wait()
    local[2].wait()
    k_core = [None] * 4
    v_core = [None] * 4
    k_y = go(remote(kbuf.at[0, low], kbuf.at[1, low], dev_ynear))
    v_z = go(remote(vbuf.at[0, low], vbuf.at[2, low], dev_znear))
    v_y = go(remote(vbuf.at[0, low], vbuf.at[1, low], dev_ynear))
    k_z = go(remote(kbuf.at[0, low], kbuf.at[2, low], dev_znear))
    k_core[0] = go(remote(kbuf.at[0, low], kbuf.at[0, high], dev_core))
    v_core[0] = go(remote(vbuf.at[0, low], vbuf.at[0, high], dev_core))

    for copy in local[3:5]:
        copy.wait()
    selfk[...] = selfk_ref[...].astype(F32)
    selfv[...] = selfv_ref[...].astype(F32)
    num[...] = jnp.zeros_like(num)
    top[...] = jnp.zeros_like(top)
    den[...] = jnp.zeros_like(den)

    def one_row(r, carry):
        rows = pl.ds(pl.multiple_of(r * 16, 16), 16)
        q = qbuf[rows, :]
        s = lax.dot_general(q, skbuf[r], (((1,), (1,)), ((), ())), preferred_element_type=F32) * scale
        live = lax.broadcasted_iota(jnp.int32, s.shape, 1) < len_ref[r]
        s = jnp.where(live, s, 0.0)
        s_self = jnp.sum(q.astype(F32) * selfk[pl.ds(r, 1), :], axis=1, keepdims=True) * scale
        m = jnp.maximum(jnp.maximum(jnp.max(s, axis=1, keepdims=True), s_self), 0.0)
        base = jnp.exp2(-m)
        shifted = jnp.where(live, jnp.exp2(s - m) - base, 0.0)
        shifted_self = jnp.exp2(s_self - m) - base
        weights = jnp.maximum(shifted, 0.0).astype(BF16)
        weight_self = jnp.maximum(shifted_self, 0.0).astype(BF16).astype(F32)
        total = jnp.dot(weights, svbuf[r], preferred_element_type=F32)
        num[rows, :] = total + weight_self * selfv[pl.ds(r, 1), :]
        size = jnp.abs(shifted)
        size = size[:, :128] + size[:, 128:]
        lane = lax.broadcasted_iota(jnp.int32, size.shape, 1)
        den[rows, :] = size + jnp.where(lane == 0, jnp.abs(shifted_self), 0.0)
        top[rows, :] = jnp.broadcast_to(m, size.shape)
        return carry

    lax.fori_loop(0, 8, one_row, 0)

    def absorb(g, i):
        rows = pl.ds(pl.multiple_of(i * TILE, TILE), TILE)
        s = lax.dot_general(
            qbuf[rows, :], kbuf[g], (((1,), (1,)), ((), ())), preferred_element_type=F32
        ) * scale
        old = top[rows, :]
        new = jnp.maximum(old, jnp.max(s, axis=1, keepdims=True))
        base = jnp.exp2(-new)
        rescale = jnp.exp2(old - new)
        size = den[rows, :] * rescale
        weights = []
        for j in range(2 * KEYS // 128):
            shifted = jnp.exp2(s[:, j * 128 : (j + 1) * 128] - new) - base
            weights.append(jnp.maximum(shifted, 0.0).astype(BF16))
            size = size + jnp.abs(shifted)
        weights = jnp.concatenate(weights, axis=1)
        total = num[rows, :] * rescale + jnp.dot(weights, vbuf[g], preferred_element_type=F32)
        return rows, new, size, total

    def stage(g):
        def tile(i, carry):
            rows, new, size, total = absorb(g, i)
            top[rows, :] = new
            den[rows, :] = size
            num[rows, :] = total
            return carry

        lax.fori_loop(0, 8 * QROWS // TILE, tile, 0)

    k_core[0].wait_recv()
    v_core[0].wait_recv()
    for copy in q_copies:
        copy.wait_recv()
    stage(0)
    k_y.wait_recv()
    k_d = go(remote(kbuf.at[1, low], kbuf.at[3, low], dev_znear))
    v_z.wait_recv()
    v_d = go(remote(vbuf.at[2, low], vbuf.at[3, low], dev_ynear))
    v_y.wait_recv()
    k_core[1] = go(remote(kbuf.at[1, low], kbuf.at[1, high], dev_core))
    v_core[1] = go(remote(vbuf.at[1, low], vbuf.at[1, high], dev_core))
    k_z.wait_recv()
    k_core[2] = go(remote(kbuf.at[2, low], kbuf.at[2, high], dev_core))
    v_core[2] = go(remote(vbuf.at[2, low], vbuf.at[2, high], dev_core))
    k_core[1].wait_recv()
    v_core[1].wait_recv()
    stage(1)
    k_core[2].wait_recv()
    v_core[2].wait_recv()
    stage(2)
    k_d.wait_recv()
    k_core[3] = go(remote(kbuf.at[3, low], kbuf.at[3, high], dev_core))
    v_d.wait_recv()
    v_core[3] = go(remote(vbuf.at[3, low], vbuf.at[3, high], dev_core))
    local[5].wait()
    w_copy = go(remote(wbuf.at[0], wbuf.at[1], dev_core))
    k_core[3].wait_recv()
    v_core[3].wait_recv()

    part_slots = [(next(slots), next(slots)) for _ in range(7)]
    first_slot = part_slots[0][0]

    def stat_rows(new, size):
        lane = lax.broadcasted_iota(jnp.int32, new.shape, 1)
        both = jnp.where(lane == 0, new, jnp.where(lane == 1, jnp.sum(size, axis=1, keepdims=True), 0.0))
        return both.T[0:8, :]

    def part_copies(r):
        rows = pl.ds(pl.multiple_of(r * QROWS, QROWS), QROWS)
        stat = pl.ds(pl.multiple_of(r * 8, 8), 8)
        to = coset(r, -1)
        slot = first_slot + 2 * (r - 1)
        return (
            remote(pn_out.at[rows], pn_in.at[rows], to, slot),
            remote(ps_out.at[stat], ps_in.at[stat], to, slot + 1),
        )

    def last(i):
        rows, new, size, total = absorb(3, i)
        pn_out[rows, :] = total.astype(BF16)
        for half in range(2):
            part = slice(half * QROWS, (half + 1) * QROWS)
            r = i * 2 + half
            ps_out[pl.ds(pl.multiple_of(r * 8, 8), 8), :] = stat_rows(new[part], size[part])
        return total

    def last_tile(step, carry):
        i = 3 - step
        last(i)
        for half in range(2):
            for copy in part_copies(i * 2 + half):
                copy.start()
        return carry

    lax.fori_loop(0, 3, last_tile, 0)
    total = last(0)
    for copy in part_copies(1):
        copy.start()
    num[pl.ds(0, QROWS), :] = total[:QROWS]

    for r in range(1, 8):
        for copy in part_copies(r):
            copy.wait_recv()
            started.append(copy)
    tops = jnp.concatenate([ps_out[0:1, :]] + [ps_in[r * 8 : r * 8 + 1, :] for r in range(1, 8)], axis=0)
    dens = jnp.concatenate([ps_out[1:2, :]] + [ps_in[r * 8 + 1 : r * 8 + 2, :] for r in range(1, 8)], axis=0)
    new = jnp.max(tops, axis=0, keepdims=True)
    rescale = jnp.exp2(tops - new)
    bottom = jnp.sum(rescale * dens, axis=0, keepdims=True) + EPS * jnp.exp2(-new)
    factor = rescale / bottom
    factor = jnp.concatenate([factor, jnp.zeros((120, 128), F32)], axis=0).T
    total = num[pl.ds(0, QROWS), :] * factor[:, 0:1]
    for r in range(1, 8):
        total = total + pn_in[pl.ds(r * QROWS, QROWS), :].astype(F32) * factor[:, r : r + 1]
    att[...] = total
    by_head = [att[pl.ds(h, 8, stride=16), :] for h in range(16)]
    own = z * NY + y
    land[own] = jnp.concatenate(by_head, axis=0).astype(BF16)

    z_copies = [None] + [go(remote(land.at[own], land.at[own], line(r))) for r in range(1, NZ)]
    arrived = {}
    for k in range(4):
        for r in range(NZ):
            zz = lax.rem(z + r, NZ)
            if k == 0 and r > 0:
                z_copies[r].wait_recv()
            for way in range(2):
                if k > 0:
                    arrived[way, k - 1, r].wait_recv()
                if k == 3 and (r < 2) != (way == 0):
                    continue
                yy = lax.rem(y + NY - k, NY) if way == 0 else lax.rem(y + k, NY)
                block = land.at[zz * NY + yy]
                arrived[way, k, r] = go(remote(block, block, dev_right if way == 0 else dev_left))
    for r in range(NZ):
        arrived[0 if r < 2 else 1, 3, r].wait_recv()

    w_copy.wait_recv()
    for j in range(8):
        pair = land[:, j * 16 : (j + 1) * 16, :].astype(F32).reshape(32, 2, 8, 128)
        for half in range(2):
            h = 2 * j + half
            rows_all[:, h * 128 : (h + 1) * 128] = pair[:, half].reshape(256, 128).astype(BF16)
    prod[0] = jnp.dot(rows_all[...], wbuf[0], preferred_element_type=F32).astype(BF16)
    prod[1] = jnp.dot(rows_all[...], wbuf[1], preferred_element_type=F32).astype(BF16)

    def piece(r):
        t = lax.rem(zh + r // 8, NZH) * NX + lax.rem(x + lax.rem(r // 2, 4), NX)
        return prod.at[r % 2, pl.ds(pl.multiple_of(t * 32, 32), 32)]

    out_copies = [go(remote(piece(r), pieces.at[r], owner(r))) for r in range(1, 16)]
    own_rows = pl.ds(pl.multiple_of((zh * NX + x) * 32, 32), 32)
    sums = [prod[0, own_rows, :].astype(F32), None]
    for r in range(1, 16):
        out_copies[r - 1].wait_recv()
        term = pieces[r].astype(F32)
        sums[r % 2] = term if sums[r % 2] is None else sums[r % 2] + term
    first = jnp.where(c == 0, sums[0], sums[1]).reshape(4, 1, 8, 256)
    second = jnp.where(c == 0, sums[1], sums[0]).reshape(4, 1, 8, 256)
    out_ref[...] = jnp.concatenate([first, second], axis=1).reshape(64, 256).astype(BF16)

    for copy in started:
        copy.wait_send()


def on_device(q, pk, pv, sk, sv, selfk, selfv, lengths, w):
    hbm = pl.BlockSpec(memory_space=pltpu.HBM)
    vmem = pltpu.VMEM
    return pl.pallas_call(
        kernel,
        out_shape=jax.ShapeDtypeStruct((64, 256), BF16),
        in_specs=[hbm] * 6 + [pl.BlockSpec(memory_space=vmem)] * 2 + [pl.BlockSpec(memory_space=pltpu.SMEM)],
        out_specs=pl.BlockSpec(memory_space=vmem),
        scratch_shapes=[
            vmem((8 * QROWS, 128), BF16),
            vmem((4, 2 * KEYS, 128), BF16),
            vmem((4, 2 * KEYS, 128), BF16),
            vmem((8, 256, 128), BF16),
            vmem((8, 256, 128), BF16),
            vmem((8, 128), F32),
            vmem((8, 128), F32),
            vmem((2, 2048, 256), BF16),
            vmem((8 * QROWS, 128), F32),
            vmem((8 * QROWS, 128), F32),
            vmem((8 * QROWS, 128), F32),
            vmem((8 * QROWS, 128), BF16),
            vmem((64, 128), F32),
            vmem((8 * QROWS, 128), BF16),
            vmem((64, 128), F32),
            vmem((QROWS, 128), F32),
            vmem((32, QROWS, 128), BF16),
            vmem((256, 2048), BF16),
            vmem((2, 256, 256), BF16),
            vmem((16, 32, 256), BF16),
            pltpu.SemaphoreType.DMA((6,)),
            pltpu.SemaphoreType.DMA((96,)),
            pltpu.SemaphoreType.DMA((96,)),
        ],
        compiler_params=pltpu.CompilerParams(
            collective_id=0, has_side_effects=True, vmem_limit_bytes=48 << 20
        ),
        name="attend_project",
    )(
        q.reshape(QROWS, 128), pk.reshape(KEYS, 128), pv.reshape(KEYS, 128),
        sk.reshape(8, 256, 128), sv.reshape(8, 256, 128), w, selfk.reshape(8, 128), selfv.reshape(8, 128), lengths,
    )


def solution(mesh):
    return jax.shard_map(
        on_device,
        mesh=mesh,
        in_specs=(
            P("seq", "tp", None),
            P("seq", "tp", None),
            P("seq", "tp", None),
            P("seq", None, "tp", None),
            P("seq", None, "tp", None),
            P("seq", "tp", None),
            P("seq", "tp", None),
            P("seq"),
            P("tp", "seq"),
        ),
        out_specs=P("tp", "seq"),
        check_vma=False,
    )
```

```python
import functools
import math

import jax
import jax.numpy as jnp
from jax import lax
from jax.experimental import pallas as pl
from jax.experimental.pallas import tpu as pltpu
from jax.sharding import PartitionSpec as P

EPS = 1e-06
MESH = pl.DeviceIdType.MESH
F32 = jnp.float32
BF16 = jnp.bfloat16

NZ, NY, NX, NZH = 4, 8, 4, 2
QROWS = 128
KEYS = 512
TILE = 256


def coordinates():
    s = lax.axis_index("seq")
    t = lax.axis_index("tp")
    return s // 16, lax.rem(s // 2, NY), lax.rem(s, 2), t // NX, lax.rem(t, NX)


def device(z, y, c, zh, x):
    return ((z * NY + y) * 2 + c, zh * NX + x)


def kernel(
    q_hbm, pk_hbm, pv_hbm, sk_hbm, sv_hbm, w_hbm, selfk_ref, selfv_ref, len_ref,
    out_ref,
    qbuf, kbuf, vbuf, skbuf, svbuf, selfk, selfv, wbuf,
    num, top, den, pn_out, ps_out, pn_in, ps_in, att, land, rows_all, prod, pieces,
    local_sem, send_sem, recv_sem, met,
):
    z, y, c, zh, x = coordinates()
    z_near = z + 1 - 2 * lax.rem(z, 2)
    other = 1 - c
    scale = math.log2(math.e) / math.sqrt(128)

    local = [
        pltpu.make_async_copy(src, dst, local_sem.at[i])
        for i, (src, dst) in enumerate(
            [
                (q_hbm, qbuf.at[pl.ds(0, QROWS)]),
                (pk_hbm, kbuf.at[0, pl.ds(0, KEYS)]),
                (pv_hbm, vbuf.at[0, pl.ds(0, KEYS)]),
                (sk_hbm, skbuf),
                (sv_hbm, svbuf),
                (w_hbm, wbuf.at[0]),
            ]
        )
    ]
    for copy in local:
        copy.start()

    dev_core = device(z, y, other, zh, x)
    dev_znear = device(z_near, y, c, zh, x)

    def coset(r, sign):
        if sign > 0:
            zz = lax.rem(z + 2 * (r // 4), NZ)
            yy = lax.rem(y + 2 * lax.rem(r, 4), NY)
        else:
            zz = lax.rem(z + NZ - 2 * (r // 4), NZ)
            yy = lax.rem(y + NY - 2 * lax.rem(r, 4), NY)
        return device(zz, yy, c, zh, x)

    def line(r):
        return device(lax.rem(z + NZ - r, NZ), y, c, zh, x)

    dev_right = device(z, lax.rem(y + 1, NY), c, zh, x)
    dev_left = device(z, lax.rem(y + NY - 1, NY), c, zh, x)

    def owner(r):
        return device(
            z, y, lax.rem(c + lax.rem(r, 2), 2), lax.rem(zh + r // 8, NZH), lax.rem(x + lax.rem(r // 2, 4), NX)
        )

    steps = [owner(1), owner(2), owner(6), owner(8)]
    partners = [dev_right, dev_left] + steps
    partners += [coset(r, 1) for r in range(1, 8)]
    partners += [line(r) for r in range(1, NZ)]
    barrier = pltpu.get_barrier_semaphore()
    for partner in partners:
        pl.semaphore_signal(barrier, inc=1, device_id=partner, device_id_type=MESH)
    pl.semaphore_wait(barrier, len(partners))

    slots = iter(range(1000))

    def remote(src, dst, to, slot=None):
        slot = next(slots) if slot is None else slot
        return pltpu.make_async_remote_copy(
            src_ref=src, dst_ref=dst, send_sem=send_sem.at[slot], recv_sem=recv_sem.at[slot],
            device_id=to, device_id_type=MESH,
        )

    started = []

    def go(copy):
        copy.start()
        started.append(copy)
        return copy

    def meet(i):
        for to in steps:
            pl.semaphore_signal(met.at[i], inc=1, device_id=to, device_id_type=MESH)

    local[0].wait()
    q_copies = [
        go(remote(qbuf.at[pl.ds(0, QROWS)], qbuf.at[pl.ds(r * QROWS, QROWS)], coset(r, 1)))
        for r in (6, 2, 5, 7, 1, 3, 4)
    ]
    low, high = pl.ds(0, KEYS), pl.ds(KEYS, KEYS)
    half_a, half_b = pl.ds(0, KEYS // 2), pl.ds(KEYS // 2, KEYS // 2)
    tail_a, tail_b = pl.ds(KEYS, KEYS // 2), pl.ds(KEYS + KEYS // 2, KEYS // 2)
    local[1].wait()
    local[2].wait()
    k_a = go(remote(kbuf.at[0, half_a], kbuf.at[1, half_a], dev_left))
    k_b = go(remote(kbuf.at[0, half_b], kbuf.at[1, half_b], dev_right))
    v_z = go(remote(vbuf.at[0, low], vbuf.at[1, high], dev_znear))
    k_core = go(remote(kbuf.at[0, low], kbuf.at[0, high], dev_core))
    v_core = go(remote(vbuf.at[0, low], vbuf.at[0, high], dev_core))
    v_a = go(remote(vbuf.at[0, half_a], vbuf.at[1, half_a], dev_left))
    v_b = go(remote(vbuf.at[0, half_b], vbuf.at[1, half_b], dev_right))
    k_z = go(remote(kbuf.at[0, low], kbuf.at[1, high], dev_znear))
    meet(0)

    for copy in local[3:5]:
        copy.wait()
    selfk[...] = selfk_ref[...].astype(F32)
    selfv[...] = selfv_ref[...].astype(F32)
    num[...] = jnp.zeros_like(num)
    top[...] = jnp.zeros_like(top)
    den[...] = jnp.zeros_like(den)

    def one_row(r, carry):
        rows = pl.ds(pl.multiple_of(r * 16, 16), 16)
        q = qbuf[rows, :]
        s = lax.dot_general(q, skbuf[r], (((1,), (1,)), ((), ())), preferred_element_type=F32) * scale
        live = lax.broadcasted_iota(jnp.int32, s.shape, 1) < len_ref[r]
        s = jnp.where(live, s, 0.0)
        s_self = jnp.sum(q.astype(F32) * selfk[pl.ds(r, 1), :], axis=1, keepdims=True) * scale
        m = jnp.maximum(jnp.maximum(jnp.max(s, axis=1, keepdims=True), s_self), 0.0)
        base = jnp.exp2(-m)
        shifted = jnp.where(live, jnp.exp2(s - m) - base, 0.0)
        shifted_self = jnp.exp2(s_self - m) - base
        weights = jnp.maximum(shifted, 0.0).astype(BF16)
        weight_self = jnp.maximum(shifted_self, 0.0).astype(BF16).astype(F32)
        total = jnp.dot(weights, svbuf[r], preferred_element_type=F32)
        num[rows, :] = total + weight_self * selfv[pl.ds(r, 1), :]
        size = jnp.abs(shifted)
        size = size[:, :128] + size[:, 128:]
        lane = lax.broadcasted_iota(jnp.int32, size.shape, 1)
        den[rows, :] = size + jnp.where(lane == 0, jnp.abs(shifted_self), 0.0)
        top[rows, :] = jnp.broadcast_to(m, size.shape)
        return carry

    lax.fori_loop(0, 8, one_row, 0)

    def absorb(g, i):
        rows = pl.ds(pl.multiple_of(i * TILE, TILE), TILE)
        s = lax.dot_general(
            qbuf[rows, :], kbuf[g], (((1,), (1,)), ((), ())), preferred_element_type=F32
        ) * scale
        old = top[rows, :]
        new = jnp.maximum(old, jnp.max(s, axis=1, keepdims=True))
        base = jnp.exp2(-new)
        rescale = jnp.exp2(old - new)
        size = den[rows, :] * rescale
        weights = []
        for j in range(2 * KEYS // 128):
            shifted = jnp.exp2(s[:, j * 128 : (j + 1) * 128] - new) - base
            weights.append(jnp.maximum(shifted, 0.0).astype(BF16))
            size = size + jnp.abs(shifted)
        weights = jnp.concatenate(weights, axis=1)
        total = num[rows, :] * rescale + jnp.dot(weights, vbuf[g], preferred_element_type=F32)
        return rows, new, size, total

    def stage(g):
        def tile(i, carry):
            rows, new, size, total = absorb(g, i)
            top[rows, :] = new
            den[rows, :] = size
            num[rows, :] = total
            return carry

        lax.fori_loop(0, 8 * QROWS // TILE, tile, 0)

    k_core.wait_recv()
    v_core.wait_recv()
    for copy in q_copies:
        copy.wait_recv()
    stage(0)
    k_a.wait_recv()
    k_b.wait_recv()
    k_d = go(remote(kbuf.at[1, low], kbuf.at[3, low], dev_znear))
    v_z.wait_recv()
    v_da = go(remote(vbuf.at[1, tail_a], vbuf.at[3, half_a], dev_left))
    v_db = go(remote(vbuf.at[1, tail_b], vbuf.at[3, half_b], dev_right))
    k_core = go(remote(kbuf.at[1, low], kbuf.at[2, low], dev_core))
    v_core = go(remote(vbuf.at[1, high], vbuf.at[2, high], dev_core))
    pl.semaphore_wait(met.at[0], len(steps))
    meet(1)
    v_a.wait_recv()
    v_b.wait_recv()
    v_core_y = go(remote(vbuf.at[1, low], vbuf.at[2, low], dev_core))
    k_z.wait_recv()
    k_core_z = go(remote(kbuf.at[1, high], kbuf.at[2, high], dev_core))
    stage(1)
    pl.semaphore_wait(met.at[1], len(steps))
    meet(2)
    k_core.wait_recv()
    v_core.wait_recv()
    v_core_y.wait_recv()
    k_core_z.wait_recv()
    k_d.wait_recv()
    k_core = go(remote(kbuf.at[3, low], kbuf.at[3, high], dev_core))
    v_da.wait_recv()
    v_db.wait_recv()
    v_core = go(remote(vbuf.at[3, low], vbuf.at[3, high], dev_core))
    stage(2)
    local[5].wait()
    w_copy = go(remote(wbuf.at[0], wbuf.at[1], dev_core))
    pl.semaphore_wait(met.at[2], len(steps))
    k_core.wait_recv()
    v_core.wait_recv()

    part_slots = [(next(slots), next(slots)) for _ in range(7)]
    first_slot = part_slots[0][0]

    def stat_rows(new, size):
        lane = lax.broadcasted_iota(jnp.int32, new.shape, 1)
        both = jnp.where(lane == 0, new, jnp.where(lane == 1, jnp.sum(size, axis=1, keepdims=True), 0.0))
        return both.T[0:8, :]

    def part_copies(r):
        rows = pl.ds(pl.multiple_of(r * QROWS, QROWS), QROWS)
        stat = pl.ds(pl.multiple_of(r * 8, 8), 8)
        to = coset(r, -1)
        slot = first_slot + 2 * (r - 1)
        return (
            remote(pn_out.at[rows], pn_in.at[rows], to, slot),
            remote(ps_out.at[stat], ps_in.at[stat], to, slot + 1),
        )

    def last(i):
        rows, new, size, total = absorb(3, i)
        pn_out[rows, :] = total.astype(BF16)
        for half in range(2):
            part = slice(half * QROWS, (half + 1) * QROWS)
            r = i * 2 + half
            ps_out[pl.ds(pl.multiple_of(r * 8, 8), 8), :] = stat_rows(new[part], size[part])
        return total

    def last_tile(step, carry):
        i = 3 - step
        last(i)
        for half in range(2):
            for copy in part_copies(i * 2 + half):
                copy.start()
        return carry

    lax.fori_loop(0, 3, last_tile, 0)
    total = last(0)
    for copy in part_copies(1):
        copy.start()
    num[pl.ds(0, QROWS), :] = total[:QROWS]

    for r in range(1, 8):
        for copy in part_copies(r):
            copy.wait_recv()
            started.append(copy)
    tops = jnp.concatenate([ps_out[0:1, :]] + [ps_in[r * 8 : r * 8 + 1, :] for r in range(1, 8)], axis=0)
    dens = jnp.concatenate([ps_out[1:2, :]] + [ps_in[r * 8 + 1 : r * 8 + 2, :] for r in range(1, 8)], axis=0)
    new = jnp.max(tops, axis=0, keepdims=True)
    rescale = jnp.exp2(tops - new)
    bottom = jnp.sum(rescale * dens, axis=0, keepdims=True) + EPS * jnp.exp2(-new)
    factor = rescale / bottom
    factor = jnp.concatenate([factor, jnp.zeros((120, 128), F32)], axis=0).T
    total = num[pl.ds(0, QROWS), :] * factor[:, 0:1]
    for r in range(1, 8):
        total = total + pn_in[pl.ds(r * QROWS, QROWS), :].astype(F32) * factor[:, r : r + 1]
    att[...] = total
    by_head = [att[pl.ds(h, 8, stride=16), :] for h in range(16)]
    own = z * NY + y
    land[own] = jnp.concatenate(by_head, axis=0).astype(BF16)

    z_copies = [None] + [go(remote(land.at[own], land.at[own], line(r))) for r in range(1, NZ)]
    ways = ((dev_right, coset(1, 1)), (dev_left, coset(1, -1)))
    near, mid, far = {}, {}, {}

    def block(r, dy):
        return land.at[lax.rem(z + r, NZ) * NY + lax.rem(y + NY + dy, NY)]

    def pass_on(r, way, dy, to):
        return go(remote(block(r, dy), block(r, dy), to))

    for r in range(NZ):
        if r > 0:
            z_copies[r].wait_recv()
        for way in range(2):
            near[r, way] = pass_on(r, way, 0, ways[way][0])
    for r in range(NZ):
        for way in range(2):
            near[r, way].wait_recv()
            mid[r, way] = pass_on(r, way, (-1, 1)[way], ways[way][0])
    for r in range(NZ):
        for way in range(2):
            mid[r, way].wait_recv()
            far[r, way] = [pass_on(r, way, (-2, 2)[way], ways[way][0])]
            if (r < 2) == (way == 0):
                far[r, way].append(pass_on(r, way, (-2, 2)[way], ways[way][1]))
    for copies in far.values():
        for copy in copies:
            copy.wait_recv()

    w_copy.wait_recv()
    for j in range(8):
        pair = land[:, j * 16 : (j + 1) * 16, :].astype(F32).reshape(32, 2, 8, 128)
        for half in range(2):
            h = 2 * j + half
            rows_all[:, h * 128 : (h + 1) * 128] = pair[:, half].reshape(256, 128).astype(BF16)
    prod[0] = jnp.dot(rows_all[...], wbuf[0], preferred_element_type=F32).astype(BF16)
    prod[1] = jnp.dot(rows_all[...], wbuf[1], preferred_element_type=F32).astype(BF16)

    def piece(r):
        t = lax.rem(zh + r // 8, NZH) * NX + lax.rem(x + lax.rem(r // 2, 4), NX)
        return prod.at[r % 2, pl.ds(pl.multiple_of(t * 32, 32), 32)]

    out_copies = [go(remote(piece(r), pieces.at[r], owner(r))) for r in range(1, 16)]
    own_rows = pl.ds(pl.multiple_of((zh * NX + x) * 32, 32), 32)
    sums = [prod[0, own_rows, :].astype(F32), None]
    for r in range(1, 16):
        out_copies[r - 1].wait_recv()
        term = pieces[r].astype(F32)
        sums[r % 2] = term if sums[r % 2] is None else sums[r % 2] + term
    first = jnp.where(c == 0, sums[0], sums[1]).reshape(4, 1, 8, 256)
    second = jnp.where(c == 0, sums[1], sums[0]).reshape(4, 1, 8, 256)
    out_ref[...] = jnp.concatenate([first, second], axis=1).reshape(64, 256).astype(BF16)

    for copy in started:
        copy.wait_send()


def on_device(q, pk, pv, sk, sv, selfk, selfv, lengths, w):
    hbm = pl.BlockSpec(memory_space=pltpu.HBM)
    vmem = pltpu.VMEM
    return pl.pallas_call(
        kernel,
        out_shape=pltpu.VMEM((64, 256), BF16),
        in_specs=[hbm] * 6 + [pl.BlockSpec(memory_space=vmem)] * 2 + [pl.BlockSpec(memory_space=pltpu.SMEM)],
        out_specs=pl.BlockSpec(memory_space=vmem),
        scratch_shapes=[
            vmem((8 * QROWS, 128), BF16),
            vmem((4, 2 * KEYS, 128), BF16),
            vmem((4, 2 * KEYS, 128), BF16),
            vmem((8, 256, 128), BF16),
            vmem((8, 256, 128), BF16),
            vmem((8, 128), F32),
            vmem((8, 128), F32),
            vmem((2, 2048, 256), BF16),
            vmem((8 * QROWS, 128), F32),
            vmem((8 * QROWS, 128), F32),
            vmem((8 * QROWS, 128), F32),
            vmem((8 * QROWS, 128), BF16),
            vmem((64, 128), F32),
            vmem((8 * QROWS, 128), BF16),
            vmem((64, 128), F32),
            vmem((QROWS, 128), F32),
            vmem((32, QROWS, 128), BF16),
            vmem((256, 2048), BF16),
            vmem((2, 256, 256), BF16),
            vmem((16, 32, 256), BF16),
            pltpu.SemaphoreType.DMA((6,)),
            pltpu.SemaphoreType.DMA((96,)),
            pltpu.SemaphoreType.DMA((96,)),
            pltpu.SemaphoreType.REGULAR((3,)),
        ],
        compiler_params=pltpu.CompilerParams(
            collective_id=0, has_side_effects=True, vmem_limit_bytes=60 << 20
        ),
        name="attend_project",
    )(
        q.reshape(QROWS, 128), pk.reshape(KEYS, 128), pv.reshape(KEYS, 128),
        sk.reshape(8, 256, 128), sv.reshape(8, 256, 128), w, selfk.reshape(8, 128), selfv.reshape(8, 128), lengths,
    )


def solution(mesh):
    return jax.shard_map(
        on_device,
        mesh=mesh,
        in_specs=(
            P("seq", "tp", None),
            P("seq", "tp", None),
            P("seq", "tp", None),
            P("seq", None, "tp", None),
            P("seq", None, "tp", None),
            P("seq", "tp", None),
            P("seq", "tp", None),
            P("seq"),
            P("tp", "seq"),
        ),
        out_specs=P("tp", "seq"),
        check_vma=False,
    )
```

```python
import functools
import math

import jax
import jax.numpy as jnp
from jax import lax
from jax.experimental import pallas as pl
from jax.experimental.pallas import tpu as pltpu
from jax.sharding import PartitionSpec as P

EPS = 1e-06
MESH = pl.DeviceIdType.MESH
F32 = jnp.float32
BF16 = jnp.bfloat16

NZ, NY, NX, NZH = 4, 8, 4, 2
QROWS = 128
KEYS = 512
TILE = 256


def coordinates():
    s = lax.axis_index("seq")
    t = lax.axis_index("tp")
    return s // 16, lax.rem(s // 2, NY), lax.rem(s, 2), t // NX, lax.rem(t, NX)


def device(z, y, c, zh, x):
    return ((z * NY + y) * 2 + c, zh * NX + x)


def kernel(
    q_hbm, pk_hbm, pv_hbm, sk_hbm, sv_hbm, w_hbm, selfk_ref, selfv_ref, len_ref,
    out_ref,
    qbuf, kbuf, vbuf, skbuf, svbuf, selfk, selfv, wbuf,
    num, top, den, pn_out, ps_out, pn_in, ps_in, att, land, rows_all, prod, pieces, scores_a, scores_b,
    local_sem, send_sem, recv_sem, met,
):
    z, y, c, zh, x = coordinates()
    z_near = z + 1 - 2 * lax.rem(z, 2)
    other = 1 - c
    scale = math.log2(math.e) / math.sqrt(128)
    scores = (scores_a, scores_b)

    local = [
        pltpu.make_async_copy(src, dst, local_sem.at[i])
        for i, (src, dst) in enumerate(
            [
                (q_hbm, qbuf.at[pl.ds(0, QROWS)]),
                (pk_hbm, kbuf.at[0, pl.ds(0, KEYS)]),
                (pv_hbm, vbuf.at[0, pl.ds(0, KEYS)]),
                (sk_hbm, skbuf),
                (sv_hbm, svbuf),
                (w_hbm, wbuf.at[0]),
            ]
        )
    ]
    for copy in local:
        copy.start()

    dev_core = device(z, y, other, zh, x)
    dev_znear = device(z_near, y, c, zh, x)

    def coset(r, sign):
        if sign > 0:
            zz = lax.rem(z + 2 * (r // 4), NZ)
            yy = lax.rem(y + 2 * lax.rem(r, 4), NY)
        else:
            zz = lax.rem(z + NZ - 2 * (r // 4), NZ)
            yy = lax.rem(y + NY - 2 * lax.rem(r, 4), NY)
        return device(zz, yy, c, zh, x)

    def z_other(m):
        return (z, z_near, lax.rem(z + 2, NZ), NZ - 1 - z)[m]

    def line(m):
        return device(z_other(m), y, c, zh, x)

    dev_right = device(z, lax.rem(y + 1, NY), c, zh, x)
    dev_left = device(z, lax.rem(y + NY - 1, NY), c, zh, x)

    def owner(r):
        return device(
            z, y, lax.rem(c + lax.rem(r, 2), 2), lax.rem(zh + r // 8, NZH), lax.rem(x + lax.rem(r // 2, 4), NX)
        )

    steps = [owner(1), owner(2), owner(6), owner(8)]
    partners = [dev_right, dev_left] + steps
    partners += [coset(r, 1) for r in range(1, 8)]
    partners += [line(r) for r in range(1, NZ)]
    barrier = pltpu.get_barrier_semaphore()
    for partner in partners:
        pl.semaphore_signal(barrier, inc=1, device_id=partner, device_id_type=MESH)
    pl.semaphore_wait(barrier, len(partners))

    slots = iter(range(1000))

    def remote(src, dst, to, slot=None):
        slot = next(slots) if slot is None else slot
        return pltpu.make_async_remote_copy(
            src_ref=src, dst_ref=dst, send_sem=send_sem.at[slot], recv_sem=recv_sem.at[slot],
            device_id=to, device_id_type=MESH,
        )

    started = []

    def go(copy):
        copy.start()
        started.append(copy)
        return copy

    def meet(i):
        for to in steps:
            pl.semaphore_signal(met.at[i], inc=1, device_id=to, device_id_type=MESH)

    local[0].wait()
    low, high = pl.ds(0, KEYS), pl.ds(KEYS, KEYS)
    half_a, half_b = pl.ds(0, KEYS // 2), pl.ds(KEYS // 2, KEYS // 2)
    tail_a, tail_b = pl.ds(KEYS, KEYS // 2), pl.ds(KEYS + KEYS // 2, KEYS // 2)
    local[1].wait()
    local[2].wait()
    q_copies = {
        r: go(remote(qbuf.at[pl.ds(0, QROWS)], qbuf.at[pl.ds(r * QROWS, QROWS)], coset(r, 1)))
        for r in (6, 2, 5, 7)
    }
    k_a = go(remote(kbuf.at[0, half_a], kbuf.at[1, half_a], dev_left))
    k_b = go(remote(kbuf.at[0, half_b], kbuf.at[1, half_b], dev_right))
    v_z = go(remote(vbuf.at[0, low], vbuf.at[1, high], dev_znear))
    q_copies.update({
        r: go(remote(qbuf.at[pl.ds(0, QROWS)], qbuf.at[pl.ds(r * QROWS, QROWS)], coset(r, 1)))
        for r in (4, 1, 3)
    })
    k_core = go(remote(kbuf.at[0, low], kbuf.at[0, high], dev_core))
    v_core = go(remote(vbuf.at[0, low], vbuf.at[0, high], dev_core))
    v_a = go(remote(vbuf.at[0, half_a], vbuf.at[1, half_a], dev_left))
    v_b = go(remote(vbuf.at[0, half_b], vbuf.at[1, half_b], dev_right))
    k_z = go(remote(kbuf.at[0, low], kbuf.at[1, high], dev_znear))
    meet(0)

    for copy in local[3:5]:
        copy.wait()
    selfk[...] = selfk_ref[...].astype(F32)
    selfv[...] = selfv_ref[...].astype(F32)
    num[...] = jnp.zeros_like(num)
    top[...] = jnp.zeros_like(top)
    den[...] = jnp.zeros_like(den)

    def one_row(r, carry):
        rows = pl.ds(pl.multiple_of(r * 16, 16), 16)
        q = qbuf[rows, :]
        s = lax.dot_general(q, skbuf[r], (((1,), (1,)), ((), ())), preferred_element_type=F32) * scale
        live = lax.broadcasted_iota(jnp.int32, s.shape, 1) < len_ref[r]
        s = jnp.where(live, s, 0.0)
        s_self = jnp.sum(q.astype(F32) * selfk[pl.ds(r, 1), :], axis=1, keepdims=True) * scale
        m = jnp.maximum(jnp.maximum(jnp.max(s, axis=1, keepdims=True), s_self), 0.0)
        base = jnp.exp2(-m)
        shifted = jnp.where(live, jnp.exp2(s - m) - base, 0.0)
        shifted_self = jnp.exp2(s_self - m) - base
        weights = jnp.maximum(shifted, 0.0).astype(BF16)
        weight_self = jnp.maximum(shifted_self, 0.0).astype(BF16).astype(F32)
        total = jnp.dot(weights, svbuf[r], preferred_element_type=F32)
        num[rows, :] = total + weight_self * selfv[pl.ds(r, 1), :]
        size = jnp.abs(shifted)
        size = size[:, :128] + size[:, 128:]
        lane = lax.broadcasted_iota(jnp.int32, size.shape, 1)
        den[rows, :] = size + jnp.where(lane == 0, jnp.abs(shifted_self), 0.0)
        top[rows, :] = jnp.broadcast_to(m, size.shape)
        return carry

    lax.fori_loop(0, 8, one_row, 0)

    def score(g, i, buf):
        rows = pl.ds(i * TILE, TILE)
        best = None
        for j in range(0, 2 * KEYS, 256):
            s = lax.dot_general(
                qbuf[rows, :], kbuf[g, j : j + 256, :], (((1,), (1,)), ((), ())), preferred_element_type=F32
            )
            buf[:, j : j + 256] = s
            s = jnp.maximum(s[:, :128], s[:, 128:])
            best = s if best is None else jnp.maximum(best, s)
        return jnp.max(best, axis=1, keepdims=True) * scale

    def absorb(g, i, buf, best):
        rows = pl.ds(i * TILE, TILE)
        old = top[rows, :]
        new = jnp.maximum(old, best)
        base = jnp.exp2(-new)
        rescale = jnp.exp2(old - new)
        size = den[rows, :] * rescale
        total = num[rows, :] * rescale
        for j in range(0, 2 * KEYS, 256):
            weights = []
            for k in range(j, j + 256, 128):
                shifted = jnp.exp2(buf[:, k : k + 128] * scale - new) - base
                weights.append(jnp.maximum(shifted, 0.0).astype(BF16))
                size = size + jnp.abs(shifted)
            weights = jnp.concatenate(weights, axis=1)
            total = total + jnp.dot(weights, vbuf[g, j : j + 256, :], preferred_element_type=F32)
        return new, size, total

    def stage(g, tiles, before, after):
        before(tiles[0])
        best = score(g, tiles[0], scores[0])
        for n, i in enumerate(tiles):
            if n + 1 < len(tiles):
                before(tiles[n + 1])
                best_next = score(g, tiles[n + 1], scores[(n + 1) % 2])
            after(i, *absorb(g, i, scores[n % 2], best))
            best = best_next

    def nothing(i):
        pass

    def keep(i, new, size, total):
        rows = pl.ds(i * TILE, TILE)
        top[rows, :] = new
        den[rows, :] = size
        num[rows, :] = total

    def await_queries(i):
        for r in (2 * i, 2 * i + 1):
            if r > 0:
                q_copies[r].wait_recv()

    def pass_near():
        k_a.wait_recv()
        k_b.wait_recv()
        k_d = go(remote(kbuf.at[1, low], kbuf.at[3, low], dev_znear))
        v_z.wait_recv()
        v_da = go(remote(vbuf.at[1, tail_a], vbuf.at[3, half_a], dev_left))
        v_db = go(remote(vbuf.at[1, tail_b], vbuf.at[3, half_b], dev_right))
        k_core_y = go(remote(kbuf.at[1, low], kbuf.at[2, low], dev_core))
        v_core_z = go(remote(vbuf.at[1, high], vbuf.at[2, high], dev_core))
        return k_d, v_da, v_db, k_core_y, v_core_z

    passed = []

    def before_first(i):
        if i == 2:
            passed.extend(pass_near())
        await_queries(i)

    k_core.wait_recv()
    v_core.wait_recv()
    stage(0, (0, 1, 2, 3), before_first, keep)
    k_d, v_da, v_db, k_core_y, v_core_z = passed
    pl.semaphore_wait(met.at[0], len(steps))
    meet(1)
    v_a.wait_recv()
    v_b.wait_recv()
    v_core_y = go(remote(vbuf.at[1, low], vbuf.at[2, low], dev_core))
    k_z.wait_recv()
    k_core_z = go(remote(kbuf.at[1, high], kbuf.at[2, high], dev_core))
    stage(1, (0, 1, 2, 3), nothing, keep)
    pl.semaphore_wait(met.at[1], len(steps))
    meet(2)
    k_core_y.wait_recv()
    v_core_z.wait_recv()
    v_core_y.wait_recv()
    k_core_z.wait_recv()
    k_d.wait_recv()
    k_core = go(remote(kbuf.at[3, low], kbuf.at[3, high], dev_core))
    v_da.wait_recv()
    v_db.wait_recv()
    v_core = go(remote(vbuf.at[3, low], vbuf.at[3, high], dev_core))
    stage(2, (0, 1, 2, 3), nothing, keep)
    local[5].wait()
    w_copy = go(remote(wbuf.at[0], wbuf.at[1], dev_core))
    pl.semaphore_wait(met.at[2], len(steps))
    k_core.wait_recv()
    v_core.wait_recv()

    part_slots = [(next(slots), next(slots)) for _ in range(7)]
    first_slot = part_slots[0][0]

    def stat_rows(new, size):
        lane = lax.broadcasted_iota(jnp.int32, new.shape, 1)
        both = jnp.where(lane == 0, new, jnp.where(lane == 1, jnp.sum(size, axis=1, keepdims=True), 0.0))
        return both.T[0:8, :]

    def part_copies(r):
        rows = pl.ds(r * QROWS, QROWS)
        stat = pl.ds(r * 8, 8)
        to = coset(r, -1)
        slot = first_slot + 2 * (r - 1)
        return (
            remote(pn_out.at[rows], pn_in.at[rows], to, slot),
            remote(ps_out.at[stat], ps_in.at[stat], to, slot + 1),
        )

    def send_parts(i, new, size, total):
        pn_out[pl.ds(i * TILE, TILE), :] = total.astype(BF16)
        for half in range(2):
            part = slice(half * QROWS, (half + 1) * QROWS)
            r = i * 2 + half
            ps_out[pl.ds(r * 8, 8), :] = stat_rows(new[part], size[part])
            if r > 0:
                for copy in part_copies(r):
                    copy.start()
        if i == 0:
            num[pl.ds(0, QROWS), :] = total[:QROWS]

    stage(3, (3, 2, 1, 0), nothing, send_parts)

    for r in range(1, 8):
        for copy in part_copies(r):
            copy.wait_recv()
            started.append(copy)
    tops = jnp.concatenate([ps_out[0:1, :]] + [ps_in[r * 8 : r * 8 + 1, :] for r in range(1, 8)], axis=0)
    dens = jnp.concatenate([ps_out[1:2, :]] + [ps_in[r * 8 + 1 : r * 8 + 2, :] for r in range(1, 8)], axis=0)
    new = jnp.max(tops, axis=0, keepdims=True)
    rescale = jnp.exp2(tops - new)
    bottom = jnp.sum(rescale * dens, axis=0, keepdims=True) + EPS * jnp.exp2(-new)
    factor = rescale / bottom
    factor = jnp.concatenate([factor, jnp.zeros((120, 128), F32)], axis=0).T
    total = num[pl.ds(0, QROWS), :] * factor[:, 0:1]
    for r in range(1, 8):
        total = total + pn_in[pl.ds(r * QROWS, QROWS), :].astype(F32) * factor[:, r : r + 1]
    att[...] = total
    by_head = [att[pl.ds(h, 8, stride=16), :] for h in range(16)]
    own = z * NY + y
    land[own] = jnp.concatenate(by_head, axis=0).astype(BF16)

    z_first = [next(slots) for _ in range(NZ)][0]

    def z_copy(m):
        return remote(land.at[own], land.at[own], line(m), z_first + m)

    for m in range(1, NZ):
        go(z_copy(m))
    ways = ((dev_right, coset(1, 1)), (dev_left, coset(1, -1)))
    near, mid, far = {}, {}, {}
    same = 1 - (z // 2 + zh - 2 * (z // 2) * zh)
    z_order = [
        z,
        same * z_other(2) + (1 - same) * z_other(1),
        same * z_other(3) + (1 - same) * z_other(2),
        same * z_other(1) + (1 - same) * z_other(3),
    ]
    bits = [0, 1 + same, 2 + same, 3 - 2 * same]

    def block(r, dy):
        return land.at[z_order[r] * NY + lax.rem(y + NY + dy, NY)]

    def pass_on(r, way, dy, to):
        return go(remote(block(r, dy), block(r, dy), to))

    def send_near(r):
        if r > 0:
            remote(land.at[own], land.at[own], dev_znear, z_first + bits[r]).wait_recv()
        for way in range(2):
            near[r, way] = pass_on(r, way, 0, ways[way][0])

    def send_mid(r):
        for way in range(2):
            near[r, way].wait_recv()
            mid[r, way] = pass_on(r, way, (-1, 1)[way], ways[way][0])

    def send_far(r):
        for way in range(2):
            mid[r, way].wait_recv()
            far[r, way] = [pass_on(r, way, (-2, 2)[way], ways[way][0])]
            if (r < 2) == (way == 0):
                far[r, way].append(pass_on(r, way, (-2, 2)[way], ways[way][1]))

    for step in (send_near, send_mid, send_far):
        for r in range(NZ):
            step(r)
    def finish_gather(r):
        for way in range(2):
            for copy in far[r, way]:
                copy.wait_recv()

    def project(side):
        first = pl.multiple_of(side * 16, 16)
        for j in range(8):
            pair = land[pl.ds(first, 16), j * 16 : (j + 1) * 16, :].astype(F32).reshape(16, 2, 8, 128)
            for half in range(2):
                h = 2 * j + half
                rows_all[:, h * 128 : (h + 1) * 128] = pair[:, half].reshape(128, 128).astype(BF16)
        rows = pl.ds(pl.multiple_of(side * 128, 128), 128)
        for core in range(2):
            prod[core, rows, :] = jnp.dot(rows_all[...], wbuf[core], preferred_element_type=F32).astype(BF16)

    def piece(r):
        t = lax.rem(zh + r // 8, NZH) * NX + lax.rem(x + lax.rem(r // 2, 4), NX)
        return prod.at[r % 2, pl.ds(pl.multiple_of(t * 32, 32), 32)]

    def send_piece(r):
        return go(remote(piece(r), pieces.at[r], owner(r)))

    for r in range(3):
        finish_gather(r)
    w_copy.wait_recv()
    project(1 - zh)
    out_copies = {r: send_piece(r) for r in (12, 13, 10, 11, 14, 15, 8, 9)}
    finish_gather(3)
    project(zh)
    out_copies.update({r: send_piece(r) for r in (4, 5, 2, 3, 6, 7, 1)})
    own_rows = pl.ds(pl.multiple_of((zh * NX + x) * 32, 32), 32)
    sums = [prod[0, own_rows, :].astype(F32), None]
    for r in range(1, 16):
        out_copies[r].wait_recv()
        term = pieces[r].astype(F32)
        sums[r % 2] = term if sums[r % 2] is None else sums[r % 2] + term
    first = jnp.where(c == 0, sums[0], sums[1]).reshape(4, 1, 8, 256)
    second = jnp.where(c == 0, sums[1], sums[0]).reshape(4, 1, 8, 256)
    out_ref[...] = jnp.concatenate([first, second], axis=1).reshape(64, 256).astype(BF16)

    for copy in started:
        copy.wait_send()


def on_device(q, pk, pv, sk, sv, selfk, selfv, lengths, w):
    hbm = pl.BlockSpec(memory_space=pltpu.HBM)
    vmem = pltpu.VMEM
    return pl.pallas_call(
        kernel,
        out_shape=pltpu.VMEM((64, 256), BF16),
        in_specs=[hbm] * 6 + [pl.BlockSpec(memory_space=vmem)] * 2 + [pl.BlockSpec(memory_space=pltpu.SMEM)],
        out_specs=pl.BlockSpec(memory_space=vmem),
        scratch_shapes=[
            vmem((8 * QROWS, 128), BF16),
            vmem((4, 2 * KEYS, 128), BF16),
            vmem((4, 2 * KEYS, 128), BF16),
            vmem((8, 256, 128), BF16),
            vmem((8, 256, 128), BF16),
            vmem((8, 128), F32),
            vmem((8, 128), F32),
            vmem((2, 2048, 256), BF16),
            vmem((8 * QROWS, 128), F32),
            vmem((8 * QROWS, 128), F32),
            vmem((8 * QROWS, 128), F32),
            vmem((8 * QROWS, 128), BF16),
            vmem((64, 128), F32),
            vmem((8 * QROWS, 128), BF16),
            vmem((64, 128), F32),
            vmem((QROWS, 128), F32),
            vmem((32, QROWS, 128), BF16),
            vmem((128, 2048), BF16),
            vmem((2, 256, 256), BF16),
            vmem((16, 32, 256), BF16),
            vmem((TILE, 2 * KEYS), F32),
            vmem((TILE, 2 * KEYS), F32),
            pltpu.SemaphoreType.DMA((6,)),
            pltpu.SemaphoreType.DMA((96,)),
            pltpu.SemaphoreType.DMA((96,)),
            pltpu.SemaphoreType.REGULAR((3,)),
        ],
        compiler_params=pltpu.CompilerParams(
            collective_id=0, has_side_effects=True, vmem_limit_bytes=60 << 20
        ),
        name="attend_project",
    )(
        q.reshape(QROWS, 128), pk.reshape(KEYS, 128), pv.reshape(KEYS, 128),
        sk.reshape(8, 256, 128), sv.reshape(8, 256, 128), w, selfk.reshape(8, 128), selfv.reshape(8, 128), lengths,
    )


def solution(mesh):
    return jax.shard_map(
        on_device,
        mesh=mesh,
        in_specs=(
            P("seq", "tp", None),
            P("seq", "tp", None),
            P("seq", "tp", None),
            P("seq", None, "tp", None),
            P("seq", None, "tp", None),
            P("seq", "tp", None),
            P("seq", "tp", None),
            P("seq"),
            P("tp", "seq"),
        ),
        out_specs=P("tp", "seq"),
        check_vma=False,
    )
```

```python
import functools
import math

import jax
import jax.numpy as jnp
from jax import lax
from jax.experimental import pallas as pl
from jax.experimental.pallas import tpu as pltpu
from jax.sharding import PartitionSpec as P

EPS = 1e-06
MESH = pl.DeviceIdType.MESH
F32 = jnp.float32
BF16 = jnp.bfloat16

NZ, NY, NX, NZH = 4, 8, 4, 2
QROWS = 128
KEYS = 512
TILE = 256


def coordinates():
    s = lax.axis_index("seq")
    t = lax.axis_index("tp")
    return s // 16, lax.rem(s // 2, NY), lax.rem(s, 2), t // NX, lax.rem(t, NX)


def device(z, y, c, zh, x):
    return ((z * NY + y) * 2 + c, zh * NX + x)


def kernel(
    q_hbm, pk_hbm, pv_hbm, sk_hbm, sv_hbm, w_hbm, selfk_ref, selfv_ref, len_ref,
    out_ref,
    qbuf, kbuf, vbuf, skbuf, svbuf, selfk, selfv, wbuf,
    num, top, den, pn_out, ps_out, pn_in, ps_in, att, land, rows_all, prod, pieces, scores_a, scores_b,
    local_sem, send_sem, recv_sem, met,
):
    z, y, c, zh, x = coordinates()
    z_near = z + 1 - 2 * lax.rem(z, 2)
    other = 1 - c
    scale = math.log2(math.e) / math.sqrt(128)
    scores = (scores_a, scores_b)

    local = [
        pltpu.make_async_copy(src, dst, local_sem.at[i])
        for i, (src, dst) in enumerate(
            [
                (q_hbm, qbuf.at[pl.ds(0, QROWS)]),
                (pk_hbm, kbuf.at[0, pl.ds(0, KEYS)]),
                (pv_hbm, vbuf.at[0, pl.ds(0, KEYS)]),
                (sk_hbm, skbuf),
                (sv_hbm, svbuf),
                (w_hbm, wbuf.at[0]),
            ]
        )
    ]
    for copy in local:
        copy.start()

    dev_core = device(z, y, other, zh, x)
    dev_znear = device(z_near, y, c, zh, x)

    def coset(r, sign):
        if sign > 0:
            zz = lax.rem(z + 2 * (r // 4), NZ)
            yy = lax.rem(y + 2 * lax.rem(r, 4), NY)
        else:
            zz = lax.rem(z + NZ - 2 * (r // 4), NZ)
            yy = lax.rem(y + NY - 2 * lax.rem(r, 4), NY)
        return device(zz, yy, c, zh, x)

    def z_other(m):
        return (z, z_near, lax.rem(z + 2, NZ), NZ - 1 - z)[m]

    def line(m):
        return device(z_other(m), y, c, zh, x)

    def along_y(d):
        return device(z, lax.rem(y + d, NY), c, zh, x)

    dev_right = device(z, lax.rem(y + 1, NY), c, zh, x)
    dev_left = device(z, lax.rem(y + NY - 1, NY), c, zh, x)

    def owner(r):
        return device(
            z, y, lax.rem(c + lax.rem(r, 2), 2), lax.rem(zh + r // 8, NZH), lax.rem(x + lax.rem(r // 2, 4), NX)
        )

    steps = [owner(1), owner(2), owner(6), owner(8)]
    partners = [dev_right, dev_left] + steps
    partners += [coset(r, 1) for r in range(1, 8)]
    partners += [line(r) for r in range(1, NZ)]
    partners += [along_y(3), along_y(5)]
    barrier = pltpu.get_barrier_semaphore()
    for partner in partners:
        pl.semaphore_signal(barrier, inc=1, device_id=partner, device_id_type=MESH)
    pl.semaphore_wait(barrier, len(partners))

    slots = iter(range(1000))

    def remote(src, dst, to, slot=None):
        slot = next(slots) if slot is None else slot
        return pltpu.make_async_remote_copy(
            src_ref=src, dst_ref=dst, send_sem=send_sem.at[slot], recv_sem=recv_sem.at[slot],
            device_id=to, device_id_type=MESH,
        )

    started = []

    def go(copy):
        copy.start()
        started.append(copy)
        return copy

    def meet(i):
        for to in steps:
            pl.semaphore_signal(met.at[i], inc=1, device_id=to, device_id_type=MESH)

    local[0].wait()
    low, high = pl.ds(0, KEYS), pl.ds(KEYS, KEYS)
    half_a, half_b = pl.ds(0, KEYS // 2), pl.ds(KEYS // 2, KEYS // 2)
    tail_a, tail_b = pl.ds(KEYS, KEYS // 2), pl.ds(KEYS + KEYS // 2, KEYS // 2)
    local[1].wait()
    local[2].wait()
    q_copies = {
        r: go(remote(qbuf.at[pl.ds(0, QROWS)], qbuf.at[pl.ds(r * QROWS, QROWS)], coset(r, 1)))
        for r in (6, 2, 5, 7)
    }
    k_a = go(remote(kbuf.at[0, half_a], kbuf.at[1, half_a], dev_left))
    k_b = go(remote(kbuf.at[0, half_b], kbuf.at[1, half_b], dev_right))
    v_z = go(remote(vbuf.at[0, low], vbuf.at[1, high], dev_znear))
    q_copies.update({
        r: go(remote(qbuf.at[pl.ds(0, QROWS)], qbuf.at[pl.ds(r * QROWS, QROWS)], coset(r, 1)))
        for r in (4, 1, 3)
    })
    k_core = go(remote(kbuf.at[0, low], kbuf.at[0, high], dev_core))
    v_core = go(remote(vbuf.at[0, low], vbuf.at[0, high], dev_core))
    v_a = go(remote(vbuf.at[0, half_a], vbuf.at[1, half_a], dev_left))
    v_b = go(remote(vbuf.at[0, half_b], vbuf.at[1, half_b], dev_right))
    k_z = go(remote(kbuf.at[0, low], kbuf.at[1, high], dev_znear))
    meet(0)

    for copy in local[3:5]:
        copy.wait()
    selfk[...] = selfk_ref[...].astype(F32)
    selfv[...] = selfv_ref[...].astype(F32)
    num[...] = jnp.zeros_like(num)
    top[...] = jnp.zeros_like(top)
    den[...] = jnp.zeros_like(den)

    own_rows = pl.ds(0, QROWS)
    q = qbuf[own_rows, :]
    by_row = [slice(r * 16, (r + 1) * 16) for r in range(8)]

    def spread(values):
        return jnp.concatenate(values, axis=0)

    s = spread([
        lax.dot_general(q[part], skbuf[r], (((1,), (1,)), ((), ())), preferred_element_type=F32)
        for r, part in enumerate(by_row)
    ]) * scale
    lengths = spread([jnp.full((16, s.shape[1]), len_ref[r], jnp.int32) for r in range(8)])
    live = lax.broadcasted_iota(jnp.int32, s.shape, 1) < lengths
    s = jnp.where(live, s, 0.0)
    own_keys = spread([jnp.broadcast_to(selfk[r : r + 1, :], (16, 128)) for r in range(8)])
    own_values = spread([jnp.broadcast_to(selfv[r : r + 1, :], (16, 128)) for r in range(8)])
    s_self = jnp.sum(q.astype(F32) * own_keys, axis=1, keepdims=True) * scale
    m = jnp.maximum(jnp.maximum(jnp.max(s, axis=1, keepdims=True), s_self), 0.0)
    base = jnp.exp2(-m)
    shifted = jnp.where(live, jnp.exp2(s - m) - base, 0.0)
    shifted_self = jnp.exp2(s_self - m) - base
    weights = jnp.maximum(shifted, 0.0).astype(BF16)
    weight_self = jnp.maximum(shifted_self, 0.0).astype(BF16).astype(F32)
    total = spread([
        jnp.dot(weights[part], svbuf[r], preferred_element_type=F32) for r, part in enumerate(by_row)
    ])
    num[own_rows, :] = total + weight_self * own_values
    size = jnp.abs(shifted)
    size = size[:, :128] + size[:, 128:]
    lane = lax.broadcasted_iota(jnp.int32, size.shape, 1)
    den[own_rows, :] = size + jnp.where(lane == 0, jnp.abs(shifted_self), 0.0)
    top[own_rows, :] = jnp.broadcast_to(m, size.shape)

    def score(g, i, buf):
        rows = pl.ds(i * TILE, TILE)
        best = None
        for j in range(0, 2 * KEYS, 256):
            s = lax.dot_general(
                qbuf[rows, :], kbuf[g, j : j + 256, :], (((1,), (1,)), ((), ())), preferred_element_type=F32
            )
            buf[:, j : j + 256] = s
            s = jnp.maximum(s[:, :128], s[:, 128:])
            best = s if best is None else jnp.maximum(best, s)
        return jnp.max(best, axis=1, keepdims=True) * scale

    def absorb(g, i, buf, best):
        rows = pl.ds(i * TILE, TILE)
        old = top[rows, :]
        new = jnp.maximum(old, best)
        base = jnp.exp2(-new)
        rescale = jnp.exp2(old - new)
        size = den[rows, :] * rescale
        total = num[rows, :] * rescale
        for j in range(0, 2 * KEYS, 256):
            weights = []
            for k in range(j, j + 256, 128):
                shifted = jnp.exp2(buf[:, k : k + 128] * scale - new) - base
                weights.append(jnp.maximum(shifted, 0.0).astype(BF16))
                size = size + jnp.abs(shifted)
            weights = jnp.concatenate(weights, axis=1)
            total = total + jnp.dot(weights, vbuf[g, j : j + 256, :], preferred_element_type=F32)
        return new, size, total

    def stage(g, tiles, before, after):
        before(tiles[0])
        best = score(g, tiles[0], scores[0])
        for n, i in enumerate(tiles):
            if n + 1 < len(tiles):
                before(tiles[n + 1])
                best_next = score(g, tiles[n + 1], scores[(n + 1) % 2])
            after(i, *absorb(g, i, scores[n % 2], best))
            best = best_next

    def nothing(i):
        pass

    def keep(i, new, size, total):
        rows = pl.ds(i * TILE, TILE)
        top[rows, :] = new
        den[rows, :] = size
        num[rows, :] = total

    def await_queries(i):
        for r in (2 * i, 2 * i + 1):
            if r > 0:
                q_copies[r].wait_recv()

    def pass_near():
        k_a.wait_recv()
        k_b.wait_recv()
        k_d = go(remote(kbuf.at[1, low], kbuf.at[3, low], dev_znear))
        v_z.wait_recv()
        v_da = go(remote(vbuf.at[1, tail_a], vbuf.at[3, half_a], dev_left))
        v_db = go(remote(vbuf.at[1, tail_b], vbuf.at[3, half_b], dev_right))
        k_core_y = go(remote(kbuf.at[1, low], kbuf.at[2, low], dev_core))
        v_core_z = go(remote(vbuf.at[1, high], vbuf.at[2, high], dev_core))
        return k_d, v_da, v_db, k_core_y, v_core_z

    passed = []

    def before_first(i):
        if i == 2:
            passed.extend(pass_near())
        await_queries(i)

    k_core.wait_recv()
    v_core.wait_recv()
    stage(0, (0, 1, 2, 3), before_first, keep)
    k_d, v_da, v_db, k_core_y, v_core_z = passed
    pl.semaphore_wait(met.at[0], len(steps))
    meet(1)
    v_a.wait_recv()
    v_b.wait_recv()
    v_core_y = go(remote(vbuf.at[1, low], vbuf.at[2, low], dev_core))
    k_z.wait_recv()
    k_core_z = go(remote(kbuf.at[1, high], kbuf.at[2, high], dev_core))
    stage(1, (0, 1, 2, 3), nothing, keep)
    pl.semaphore_wait(met.at[1], len(steps))
    meet(2)
    k_core_y.wait_recv()
    v_core_z.wait_recv()
    v_core_y.wait_recv()
    k_core_z.wait_recv()
    k_d.wait_recv()
    k_core = go(remote(kbuf.at[3, low], kbuf.at[3, high], dev_core))
    v_da.wait_recv()
    v_db.wait_recv()
    v_core = go(remote(vbuf.at[3, low], vbuf.at[3, high], dev_core))
    stage(2, (0, 1, 2, 3), nothing, keep)
    local[5].wait()
    w_copy = go(remote(wbuf.at[0], wbuf.at[1], dev_core))
    pl.semaphore_wait(met.at[2], len(steps))
    k_core.wait_recv()
    v_core.wait_recv()

    part_slots = [(next(slots), next(slots)) for _ in range(7)]
    first_slot = part_slots[0][0]

    def stat_rows(new, size):
        lane = lax.broadcasted_iota(jnp.int32, new.shape, 1)
        both = jnp.where(lane == 0, new, jnp.where(lane == 1, jnp.sum(size, axis=1, keepdims=True), 0.0))
        return both.T[0:8, :]

    def part_copies(r):
        rows = pl.ds(r * QROWS, QROWS)
        stat = pl.ds(r * 8, 8)
        to = coset(r, -1)
        slot = first_slot + 2 * (r - 1)
        return (
            remote(pn_out.at[rows], pn_in.at[rows], to, slot),
            remote(ps_out.at[stat], ps_in.at[stat], to, slot + 1),
        )

    def send_parts(i, new, size, total):
        pn_out[pl.ds(i * TILE, TILE), :] = total.astype(BF16)
        for half in range(2):
            part = slice(half * QROWS, (half + 1) * QROWS)
            r = i * 2 + half
            ps_out[pl.ds(r * 8, 8), :] = stat_rows(new[part], size[part])
            if r > 0:
                for copy in part_copies(r):
                    copy.start()
        if i == 0:
            num[pl.ds(0, QROWS), :] = total[:QROWS]

    stage(3, (3, 2, 1, 0), nothing, send_parts)

    for r in range(1, 8):
        for copy in part_copies(r):
            copy.wait_recv()
            started.append(copy)
    tops = jnp.concatenate([ps_out[0:1, :]] + [ps_in[r * 8 : r * 8 + 1, :] for r in range(1, 8)], axis=0)
    dens = jnp.concatenate([ps_out[1:2, :]] + [ps_in[r * 8 + 1 : r * 8 + 2, :] for r in range(1, 8)], axis=0)
    new = jnp.max(tops, axis=0, keepdims=True)
    rescale = jnp.exp2(tops - new)
    bottom = jnp.sum(rescale * dens, axis=0, keepdims=True) + EPS * jnp.exp2(-new)
    factor = rescale / bottom
    factor = jnp.concatenate([factor, jnp.zeros((120, 128), F32)], axis=0).T
    total = num[pl.ds(0, QROWS), :] * factor[:, 0:1]
    for r in range(1, 8):
        total = total + pn_in[pl.ds(r * QROWS, QROWS), :].astype(F32) * factor[:, r : r + 1]
    att[...] = total
    by_head = [att[pl.ds(h, 8, stride=16), :] for h in range(16)]
    own = z * NY + y
    land[own] = jnp.concatenate(by_head, axis=0).astype(BF16)

    heads_y, heads_z = pl.ds(0, 32), pl.ds(32, 96)
    z_first = [next(slots) for _ in range(NZ)][0]
    line_first = [next(slots) for _ in range(NZ)][0]

    def z_copy(m):
        return remote(land.at[own, heads_z], land.at[own, heads_z], line(m), z_first + m)

    def line_copy(m):
        whole = land.at[pl.ds(pl.multiple_of(z * NY, NY), NY), heads_y]
        return remote(whole, whole, line(m), line_first + m)

    for m in range(1, NZ):
        go(z_copy(m))
    ways = ((dev_right, coset(1, 1)), (dev_left, coset(1, -1)))
    near, mid, far = {}, {}, {}
    same = 1 - (z // 2 + zh - 2 * (z // 2) * zh)
    z_order = [
        z,
        same * z_other(2) + (1 - same) * z_other(1),
        same * z_other(3) + (1 - same) * z_other(2),
        same * z_other(1) + (1 - same) * z_other(3),
    ]
    bits = [0, 1 + same, 2 + same, 3 - 2 * same]

    def block(r, dy):
        return land.at[z_order[r] * NY + lax.rem(y + NY + dy, NY), heads_z]

    def pass_on(r, way, dy, to):
        return go(remote(block(r, dy), block(r, dy), to))

    def send_near(r):
        if r > 0:
            remote(land.at[own, heads_z], land.at[own, heads_z], dev_znear, z_first + bits[r]).wait_recv()
        for way in range(2):
            near[r, way] = pass_on(r, way, 0, ways[way][0])

    def send_mid(r):
        for way in range(2):
            near[r, way].wait_recv()
            mid[r, way] = pass_on(r, way, (-1, 1)[way], ways[way][0])

    def send_far(r):
        for way in range(2):
            mid[r, way].wait_recv()
            far[r, way] = [pass_on(r, way, (-2, 2)[way], ways[way][0])]
            if (r < 2) == (way == 0):
                far[r, way].append(pass_on(r, way, (-2, 2)[way], ways[way][1]))

    send_near(0)
    y_copies = [
        go(remote(land.at[own, heads_y], land.at[own, heads_y], along_y(d))) for d in (4, 3, 5, 2, 6, 1, 7)
    ]
    for r in range(1, NZ):
        send_near(r)
    send_mid(0)
    for copy in y_copies:
        copy.wait_recv()
    for m in range(1, NZ):
        go(line_copy(m))
    for r in range(1, NZ):
        send_mid(r)
    for r in range(NZ):
        send_far(r)

    def finish_gather(r):
        if r > 0:
            whole = land.at[pl.ds(pl.multiple_of(z * NY, NY), NY), heads_y]
            remote(whole, whole, dev_znear, line_first + bits[r]).wait_recv()
        for way in range(2):
            for copy in far[r, way]:
                copy.wait_recv()

    def project(side):
        first = pl.multiple_of(side * 16, 16)
        for j in range(8):
            pair = land[pl.ds(first, 16), j * 16 : (j + 1) * 16, :].astype(F32).reshape(16, 2, 8, 128)
            for half in range(2):
                h = 2 * j + half
                rows_all[:, h * 128 : (h + 1) * 128] = pair[:, half].reshape(128, 128).astype(BF16)
        rows = pl.ds(pl.multiple_of(side * 128, 128), 128)
        for core in range(2):
            prod[core, rows, :] = jnp.dot(rows_all[...], wbuf[core], preferred_element_type=F32).astype(BF16)

    def piece(r):
        t = lax.rem(zh + r // 8, NZH) * NX + lax.rem(x + lax.rem(r // 2, 4), NX)
        return prod.at[r % 2, pl.ds(pl.multiple_of(t * 32, 32), 32)]

    def send_piece(r):
        return go(remote(piece(r), pieces.at[r], owner(r)))

    for r in range(3):
        finish_gather(r)
    w_copy.wait_recv()
    project(1 - zh)
    out_copies = {r: send_piece(r) for r in (12, 13, 10, 11, 14, 15, 8, 9)}
    finish_gather(3)
    project(zh)
    out_copies.update({r: send_piece(r) for r in (4, 5, 2, 3, 6, 7, 1)})
    own_rows = pl.ds(pl.multiple_of((zh * NX + x) * 32, 32), 32)
    sums = [prod[0, own_rows, :].astype(F32), None]
    for r in range(1, 16):
        out_copies[r].wait_recv()
        term = pieces[r].astype(F32)
        sums[r % 2] = term if sums[r % 2] is None else sums[r % 2] + term
    first = jnp.where(c == 0, sums[0], sums[1]).reshape(4, 1, 8, 256)
    second = jnp.where(c == 0, sums[1], sums[0]).reshape(4, 1, 8, 256)
    out_ref[...] = jnp.concatenate([first, second], axis=1).reshape(64, 256).astype(BF16)

    for copy in started:
        copy.wait_send()


def on_device(q, pk, pv, sk, sv, selfk, selfv, lengths, w):
    hbm = pl.BlockSpec(memory_space=pltpu.HBM)
    vmem = pltpu.VMEM
    return pl.pallas_call(
        kernel,
        out_shape=pltpu.VMEM((64, 256), BF16),
        in_specs=[hbm] * 6 + [pl.BlockSpec(memory_space=vmem)] * 2 + [pl.BlockSpec(memory_space=pltpu.SMEM)],
        out_specs=pl.BlockSpec(memory_space=vmem),
        scratch_shapes=[
            vmem((8 * QROWS, 128), BF16),
            vmem((4, 2 * KEYS, 128), BF16),
            vmem((4, 2 * KEYS, 128), BF16),
            vmem((8, 256, 128), BF16),
            vmem((8, 256, 128), BF16),
            vmem((8, 128), F32),
            vmem((8, 128), F32),
            vmem((2, 2048, 256), BF16),
            vmem((8 * QROWS, 128), F32),
            vmem((8 * QROWS, 128), F32),
            vmem((8 * QROWS, 128), F32),
            vmem((8 * QROWS, 128), BF16),
            vmem((64, 128), F32),
            vmem((8 * QROWS, 128), BF16),
            vmem((64, 128), F32),
            vmem((QROWS, 128), F32),
            vmem((32, QROWS, 128), BF16),
            vmem((128, 2048), BF16),
            vmem((2, 256, 256), BF16),
            vmem((16, 32, 256), BF16),
            vmem((TILE, 2 * KEYS), F32),
            vmem((TILE, 2 * KEYS), F32),
            pltpu.SemaphoreType.DMA((6,)),
            pltpu.SemaphoreType.DMA((128,)),
            pltpu.SemaphoreType.DMA((128,)),
            pltpu.SemaphoreType.REGULAR((3,)),
        ],
        compiler_params=pltpu.CompilerParams(
            collective_id=0, has_side_effects=True, vmem_limit_bytes=60 << 20
        ),
        name="attend_project",
    )(
        q.reshape(QROWS, 128), pk.reshape(KEYS, 128), pv.reshape(KEYS, 128),
        sk.reshape(8, 256, 128), sv.reshape(8, 256, 128), w, selfk.reshape(8, 128), selfv.reshape(8, 128), lengths,
    )


def solution(mesh):
    return jax.shard_map(
        on_device,
        mesh=mesh,
        in_specs=(
            P("seq", "tp", None),
            P("seq", "tp", None),
            P("seq", "tp", None),
            P("seq", None, "tp", None),
            P("seq", None, "tp", None),
            P("seq", "tp", None),
            P("seq", "tp", None),
            P("seq"),
            P("tp", "seq"),
        ),
        out_specs=P("tp", "seq"),
        check_vma=False,
    )
```

```python
import functools
import math

import jax
import jax.numpy as jnp
from jax import lax
from jax.experimental import pallas as pl
from jax.experimental.pallas import tpu as pltpu
from jax.sharding import PartitionSpec as P

EPS = 1e-06
MESH = pl.DeviceIdType.MESH
F32 = jnp.float32
BF16 = jnp.bfloat16

NZ, NY, NX, NZH = 4, 8, 4, 2
QROWS = 128
KEYS = 512
TILE = 256


def coordinates():
    s = lax.axis_index("seq")
    t = lax.axis_index("tp")
    return s // 16, lax.rem(s // 2, NY), lax.rem(s, 2), t // NX, lax.rem(t, NX)


def device(z, y, c, zh, x):
    return ((z * NY + y) * 2 + c, zh * NX + x)


def kernel(
    q_hbm, pk_hbm, pv_hbm, sk_hbm, sv_hbm, w_hbm, selfk_ref, selfv_ref, len_ref,
    out_ref,
    qbuf, kbuf, vbuf, skbuf, svbuf, selfk, selfv, wbuf,
    num, top, den, pn_out, ps_out, pn_in, ps_in, att, land, rows_all, prod, pieces, scores_a, scores_b,
    local_sem, send_sem, recv_sem, met,
):
    z, y, c, zh, x = coordinates()
    z_near = z + 1 - 2 * lax.rem(z, 2)
    other = 1 - c
    scale = math.log2(math.e) / math.sqrt(128)
    scores = (scores_a, scores_b)

    local = [
        pltpu.make_async_copy(src, dst, local_sem.at[i])
        for i, (src, dst) in enumerate(
            [
                (q_hbm, qbuf.at[pl.ds(0, QROWS)]),
                (pk_hbm, kbuf.at[0, pl.ds(0, KEYS)]),
                (pv_hbm, vbuf.at[0, pl.ds(0, KEYS)]),
                (sk_hbm, skbuf),
                (sv_hbm, svbuf),
                (w_hbm, wbuf.at[0]),
            ]
        )
    ]
    for copy in local:
        copy.start()

    dev_core = device(z, y, other, zh, x)
    dev_znear = device(z_near, y, c, zh, x)

    def coset(r, sign):
        if sign > 0:
            zz = lax.rem(z + 2 * (r // 4), NZ)
            yy = lax.rem(y + 2 * lax.rem(r, 4), NY)
        else:
            zz = lax.rem(z + NZ - 2 * (r // 4), NZ)
            yy = lax.rem(y + NY - 2 * lax.rem(r, 4), NY)
        return device(zz, yy, c, zh, x)

    def z_other(m):
        return (z, z_near, lax.rem(z + 2, NZ), NZ - 1 - z)[m]

    def line(m):
        return device(z_other(m), y, c, zh, x)

    def along_y(d):
        return device(z, lax.rem(y + d, NY), c, zh, x)

    dev_right = device(z, lax.rem(y + 1, NY), c, zh, x)
    dev_left = device(z, lax.rem(y + NY - 1, NY), c, zh, x)

    def owner(r):
        return device(
            z, y, lax.rem(c + lax.rem(r, 2), 2), lax.rem(zh + r // 8, NZH), lax.rem(x + lax.rem(r // 2, 4), NX)
        )

    steps = [owner(1), owner(2), owner(6), owner(8)]
    partners = [dev_right, dev_left] + steps
    partners += [coset(r, 1) for r in range(1, 8)]
    partners += [line(r) for r in range(1, NZ)]
    partners += [along_y(3), along_y(5)]
    barrier = pltpu.get_barrier_semaphore()
    for partner in partners:
        pl.semaphore_signal(barrier, inc=1, device_id=partner, device_id_type=MESH)
    pl.semaphore_wait(barrier, len(partners))

    slots = iter(range(1000))

    def remote(src, dst, to, slot=None):
        slot = next(slots) if slot is None else slot
        return pltpu.make_async_remote_copy(
            src_ref=src, dst_ref=dst, send_sem=send_sem.at[slot], recv_sem=recv_sem.at[slot],
            device_id=to, device_id_type=MESH,
        )

    started = []

    def go(copy):
        copy.start()
        started.append(copy)
        return copy

    def meet(i):
        for to in steps:
            pl.semaphore_signal(met.at[i], inc=1, device_id=to, device_id_type=MESH)

    local[0].wait()
    low, high = pl.ds(0, KEYS), pl.ds(KEYS, KEYS)
    half_a, half_b = pl.ds(0, KEYS // 2), pl.ds(KEYS // 2, KEYS // 2)
    tail_a, tail_b = pl.ds(KEYS, KEYS // 2), pl.ds(KEYS + KEYS // 2, KEYS // 2)
    local[1].wait()
    local[2].wait()
    q_copies = {
        r: go(remote(qbuf.at[pl.ds(0, QROWS)], qbuf.at[pl.ds(r * QROWS, QROWS)], coset(r, 1)))
        for r in (6, 2, 5, 7)
    }
    k_a = go(remote(kbuf.at[0, half_a], kbuf.at[1, half_a], dev_left))
    k_b = go(remote(kbuf.at[0, half_b], kbuf.at[1, half_b], dev_right))
    v_z = go(remote(vbuf.at[0, low], vbuf.at[1, high], dev_znear))
    q_copies.update({
        r: go(remote(qbuf.at[pl.ds(0, QROWS)], qbuf.at[pl.ds(r * QROWS, QROWS)], coset(r, 1)))
        for r in (4, 1, 3)
    })
    k_core = go(remote(kbuf.at[0, low], kbuf.at[0, high], dev_core))
    v_core = go(remote(vbuf.at[0, low], vbuf.at[0, high], dev_core))
    v_a = go(remote(vbuf.at[0, half_a], vbuf.at[1, half_a], dev_left))
    v_b = go(remote(vbuf.at[0, half_b], vbuf.at[1, half_b], dev_right))
    k_z = go(remote(kbuf.at[0, low], kbuf.at[1, high], dev_znear))
    meet(0)

    for copy in local[3:5]:
        copy.wait()
    selfk[...] = selfk_ref[...].astype(F32)
    selfv[...] = selfv_ref[...].astype(F32)
    num[...] = jnp.zeros_like(num)
    top[...] = jnp.zeros_like(top)
    den[...] = jnp.zeros_like(den)

    own_rows = pl.ds(0, QROWS)
    q = qbuf[own_rows, :]
    by_row = [slice(r * 16, (r + 1) * 16) for r in range(8)]

    def spread(values):
        return jnp.concatenate(values, axis=0)

    s = spread([
        lax.dot_general(q[part], skbuf[r], (((1,), (1,)), ((), ())), preferred_element_type=F32)
        for r, part in enumerate(by_row)
    ]) * scale
    lengths = spread([jnp.full((16, s.shape[1]), len_ref[r], jnp.int32) for r in range(8)])
    live = lax.broadcasted_iota(jnp.int32, s.shape, 1) < lengths
    s = jnp.where(live, s, 0.0)
    own_keys = spread([jnp.broadcast_to(selfk[r : r + 1, :], (16, 128)) for r in range(8)])
    own_values = spread([jnp.broadcast_to(selfv[r : r + 1, :], (16, 128)) for r in range(8)])
    s_self = jnp.sum(q.astype(F32) * own_keys, axis=1, keepdims=True) * scale
    m = jnp.maximum(jnp.maximum(jnp.max(s, axis=1, keepdims=True), s_self), 0.0)
    base = jnp.exp2(-m)
    shifted = jnp.where(live, jnp.exp2(s - m) - base, 0.0)
    shifted_self = jnp.exp2(s_self - m) - base
    weights = jnp.maximum(shifted, 0.0).astype(BF16)
    weight_self = jnp.maximum(shifted_self, 0.0).astype(BF16).astype(F32)
    total = spread([
        jnp.dot(weights[part], svbuf[r], preferred_element_type=F32) for r, part in enumerate(by_row)
    ])
    num[own_rows, :] = total + weight_self * own_values
    size = jnp.abs(shifted)
    size = size[:, :128] + size[:, 128:]
    lane = lax.broadcasted_iota(jnp.int32, size.shape, 1)
    den[own_rows, :] = size + jnp.where(lane == 0, jnp.abs(shifted_self), 0.0)
    top[own_rows, :] = jnp.broadcast_to(m, size.shape)

    def score(g, i, buf):
        rows = pl.ds(i * TILE, TILE)
        best = None
        for j in range(0, 2 * KEYS, 256):
            s = lax.dot_general(
                qbuf[rows, :], kbuf[g, j : j + 256, :], (((1,), (1,)), ((), ())), preferred_element_type=F32
            )
            buf[:, j : j + 256] = s
            s = jnp.maximum(s[:, :128], s[:, 128:])
            best = s if best is None else jnp.maximum(best, s)
        return jnp.max(best, axis=1, keepdims=True) * scale

    def absorb(g, i, buf, best):
        rows = pl.ds(i * TILE, TILE)
        old = top[rows, :]
        new = jnp.maximum(old, best)
        base = jnp.exp2(-new)
        rescale = jnp.exp2(old - new)
        size = den[rows, :] * rescale
        total = num[rows, :] * rescale
        for j in range(0, 2 * KEYS, 256):
            weights = []
            for k in range(j, j + 256, 128):
                shifted = jnp.exp2(buf[:, k : k + 128] * scale - new) - base
                weights.append(jnp.maximum(shifted, 0.0).astype(BF16))
                size = size + jnp.abs(shifted)
            weights = jnp.concatenate(weights, axis=1)
            total = total + jnp.dot(weights, vbuf[g, j : j + 256, :], preferred_element_type=F32)
        return new, size, total

    def stage(g, tiles, before, after):
        before(tiles[0])
        best = score(g, tiles[0], scores[0])
        for n, i in enumerate(tiles):
            if n + 1 < len(tiles):
                before(tiles[n + 1])
                best_next = score(g, tiles[n + 1], scores[(n + 1) % 2])
            after(i, *absorb(g, i, scores[n % 2], best))
            best = best_next

    def nothing(i):
        pass

    def keep(i, new, size, total):
        rows = pl.ds(i * TILE, TILE)
        top[rows, :] = new
        den[rows, :] = size
        num[rows, :] = total

    def await_queries(i):
        for r in (2 * i, 2 * i + 1):
            if r > 0:
                q_copies[r].wait_recv()

    def pass_near():
        k_a.wait_recv()
        k_b.wait_recv()
        k_d = go(remote(kbuf.at[1, low], kbuf.at[3, low], dev_znear))
        v_z.wait_recv()
        v_da = go(remote(vbuf.at[1, tail_a], vbuf.at[3, half_a], dev_left))
        v_db = go(remote(vbuf.at[1, tail_b], vbuf.at[3, half_b], dev_right))
        k_core_y = go(remote(kbuf.at[1, low], kbuf.at[2, low], dev_core))
        v_core_z = go(remote(vbuf.at[1, high], vbuf.at[2, high], dev_core))
        return k_d, v_da, v_db, k_core_y, v_core_z

    passed = []

    def before_first(i):
        if i == 0:
            passed.extend(pass_near())
        await_queries(i)

    k_core.wait_recv()
    v_core.wait_recv()
    stage(0, (0, 1, 2, 3), before_first, keep)
    k_d, v_da, v_db, k_core_y, v_core_z = passed
    pl.semaphore_wait(met.at[0], len(steps))
    meet(1)
    v_a.wait_recv()
    v_b.wait_recv()
    v_core_y = go(remote(vbuf.at[1, low], vbuf.at[2, low], dev_core))
    k_z.wait_recv()
    k_core_z = go(remote(kbuf.at[1, high], kbuf.at[2, high], dev_core))
    stage(1, (0, 1, 2, 3), nothing, keep)
    pl.semaphore_wait(met.at[1], len(steps))
    meet(2)
    k_core_y.wait_recv()
    v_core_z.wait_recv()
    v_core_y.wait_recv()
    k_core_z.wait_recv()
    k_d.wait_recv()
    k_core = go(remote(kbuf.at[3, low], kbuf.at[3, high], dev_core))
    v_da.wait_recv()
    v_db.wait_recv()
    v_core = go(remote(vbuf.at[3, low], vbuf.at[3, high], dev_core))
    stage(2, (0, 1, 2, 3), nothing, keep)
    local[5].wait()
    w_copy = go(remote(wbuf.at[0], wbuf.at[1], dev_core))
    pl.semaphore_wait(met.at[2], len(steps))
    k_core.wait_recv()
    v_core.wait_recv()

    part_slots = [(next(slots), next(slots)) for _ in range(7)]
    first_slot = part_slots[0][0]

    def stat_rows(new, size):
        lane = lax.broadcasted_iota(jnp.int32, new.shape, 1)
        both = jnp.where(lane == 0, new, jnp.where(lane == 1, jnp.sum(size, axis=1, keepdims=True), 0.0))
        return both.T[0:8, :]

    def part_copies(r):
        rows = pl.ds(r * QROWS, QROWS)
        stat = pl.ds(r * 8, 8)
        to = coset(r, -1)
        slot = first_slot + 2 * (r - 1)
        return (
            remote(pn_out.at[rows], pn_in.at[rows], to, slot),
            remote(ps_out.at[stat], ps_in.at[stat], to, slot + 1),
        )

    def send_parts(i, new, size, total):
        pn_out[pl.ds(i * TILE, TILE), :] = total.astype(BF16)
        for half in range(2):
            part = slice(half * QROWS, (half + 1) * QROWS)
            r = i * 2 + half
            ps_out[pl.ds(r * 8, 8), :] = stat_rows(new[part], size[part])
            if r > 0:
                for copy in part_copies(r):
                    copy.start()
        if i == 0:
            num[pl.ds(0, QROWS), :] = total[:QROWS]

    stage(3, (3, 2, 1, 0), nothing, send_parts)

    for r in range(1, 8):
        for copy in part_copies(r):
            copy.wait_recv()
            started.append(copy)
    tops = jnp.concatenate([ps_out[0:1, :]] + [ps_in[r * 8 : r * 8 + 1, :] for r in range(1, 8)], axis=0)
    dens = jnp.concatenate([ps_out[1:2, :]] + [ps_in[r * 8 + 1 : r * 8 + 2, :] for r in range(1, 8)], axis=0)
    new = jnp.max(tops, axis=0, keepdims=True)
    rescale = jnp.exp2(tops - new)
    bottom = jnp.sum(rescale * dens, axis=0, keepdims=True) + EPS * jnp.exp2(-new)
    factor = rescale / bottom
    factor = jnp.concatenate([factor, jnp.zeros((120, 128), F32)], axis=0).T
    total = num[pl.ds(0, QROWS), :] * factor[:, 0:1]
    for r in range(1, 8):
        total = total + pn_in[pl.ds(r * QROWS, QROWS), :].astype(F32) * factor[:, r : r + 1]
    att[...] = total
    by_head = [att[pl.ds(h, 8, stride=16), :] for h in range(16)]
    own = z * NY + y
    land[own] = jnp.concatenate(by_head, axis=0).astype(BF16)

    heads_y, heads_z = pl.ds(0, 32), pl.ds(32, 96)
    z_first = [next(slots) for _ in range(NZ)][0]
    line_first = [next(slots) for _ in range(NZ)][0]

    def z_copy(m):
        return remote(land.at[own, heads_z], land.at[own, heads_z], line(m), z_first + m)

    def line_copy(m):
        whole = land.at[pl.ds(pl.multiple_of(z * NY, NY), NY), heads_y]
        return remote(whole, whole, line(m), line_first + m)

    for m in range(1, NZ):
        go(z_copy(m))
    ways = ((dev_right, coset(1, 1)), (dev_left, coset(1, -1)))
    near, mid, far = {}, {}, {}
    same = 1 - (z // 2 + zh - 2 * (z // 2) * zh)
    z_order = [
        z,
        same * z_other(2) + (1 - same) * z_other(1),
        same * z_other(3) + (1 - same) * z_other(2),
        same * z_other(1) + (1 - same) * z_other(3),
    ]
    bits = [0, 1 + same, 2 + same, 3 - 2 * same]

    def block(r, dy):
        return land.at[z_order[r] * NY + lax.rem(y + NY + dy, NY), heads_z]

    def pass_on(r, way, dy, to):
        return go(remote(block(r, dy), block(r, dy), to))

    def send_near(r):
        if r > 0:
            remote(land.at[own, heads_z], land.at[own, heads_z], dev_znear, z_first + bits[r]).wait_recv()
        for way in range(2):
            near[r, way] = pass_on(r, way, 0, ways[way][0])

    def send_mid(r):
        for way in range(2):
            near[r, way].wait_recv()
            mid[r, way] = pass_on(r, way, (-1, 1)[way], ways[way][0])

    def send_far(r):
        for way in range(2):
            mid[r, way].wait_recv()
            far[r, way] = [pass_on(r, way, (-2, 2)[way], ways[way][0])]
            if (r < 2) == (way == 0):
                far[r, way].append(pass_on(r, way, (-2, 2)[way], ways[way][1]))

    send_near(0)
    y_copies = [
        go(remote(land.at[own, heads_y], land.at[own, heads_y], along_y(d))) for d in (4, 3, 5, 2, 6, 1, 7)
    ]
    for r in range(1, NZ):
        send_near(r)
    send_mid(0)
    for copy in y_copies:
        copy.wait_recv()
    for m in range(1, NZ):
        go(line_copy(m))
    for r in range(1, NZ):
        send_mid(r)
    for r in range(NZ):
        send_far(r)

    def finish_gather(r):
        if r > 0:
            whole = land.at[pl.ds(pl.multiple_of(z * NY, NY), NY), heads_y]
            remote(whole, whole, dev_znear, line_first + bits[r]).wait_recv()
        for way in range(2):
            for copy in far[r, way]:
                copy.wait_recv()

    def project(side):
        first = pl.multiple_of(side * 16, 16)
        for j in range(8):
            pair = land[pl.ds(first, 16), j * 16 : (j + 1) * 16, :].astype(F32).reshape(16, 2, 8, 128)
            for half in range(2):
                h = 2 * j + half
                rows_all[:, h * 128 : (h + 1) * 128] = pair[:, half].reshape(128, 128).astype(BF16)
        rows = pl.ds(pl.multiple_of(side * 128, 128), 128)
        for core in range(2):
            prod[core, rows, :] = jnp.dot(rows_all[...], wbuf[core], preferred_element_type=F32).astype(BF16)

    def piece(r):
        t = lax.rem(zh + r // 8, NZH) * NX + lax.rem(x + lax.rem(r // 2, 4), NX)
        return prod.at[r % 2, pl.ds(pl.multiple_of(t * 32, 32), 32)]

    def send_piece(r):
        return go(remote(piece(r), pieces.at[r], owner(r)))

    for r in range(3):
        finish_gather(r)
    w_copy.wait_recv()
    project(1 - zh)
    out_copies = {r: send_piece(r) for r in (12, 13, 10, 11, 14, 15, 8, 9)}
    finish_gather(3)
    project(zh)
    out_copies.update({r: send_piece(r) for r in (4, 5, 2, 3, 6, 7, 1)})
    own_rows = pl.ds(pl.multiple_of((zh * NX + x) * 32, 32), 32)
    sums = [prod[0, own_rows, :].astype(F32), None]
    for r in range(1, 16):
        out_copies[r].wait_recv()
        term = pieces[r].astype(F32)
        sums[r % 2] = term if sums[r % 2] is None else sums[r % 2] + term
    first = jnp.where(c == 0, sums[0], sums[1]).reshape(4, 1, 8, 256)
    second = jnp.where(c == 0, sums[1], sums[0]).reshape(4, 1, 8, 256)
    out_ref[...] = jnp.concatenate([first, second], axis=1).reshape(64, 256).astype(BF16)

    for copy in started:
        copy.wait_send()


def on_device(q, pk, pv, sk, sv, selfk, selfv, lengths, w):
    hbm = pl.BlockSpec(memory_space=pltpu.HBM)
    vmem = pltpu.VMEM
    return pl.pallas_call(
        kernel,
        out_shape=pltpu.VMEM((64, 256), BF16),
        in_specs=[hbm] * 6 + [pl.BlockSpec(memory_space=vmem)] * 2 + [pl.BlockSpec(memory_space=pltpu.SMEM)],
        out_specs=pl.BlockSpec(memory_space=vmem),
        scratch_shapes=[
            vmem((8 * QROWS, 128), BF16),
            vmem((4, 2 * KEYS, 128), BF16),
            vmem((4, 2 * KEYS, 128), BF16),
            vmem((8, 256, 128), BF16),
            vmem((8, 256, 128), BF16),
            vmem((8, 128), F32),
            vmem((8, 128), F32),
            vmem((2, 2048, 256), BF16),
            vmem((8 * QROWS, 128), F32),
            vmem((8 * QROWS, 128), F32),
            vmem((8 * QROWS, 128), F32),
            vmem((8 * QROWS, 128), BF16),
            vmem((64, 128), F32),
            vmem((8 * QROWS, 128), BF16),
            vmem((64, 128), F32),
            vmem((QROWS, 128), F32),
            vmem((32, QROWS, 128), BF16),
            vmem((128, 2048), BF16),
            vmem((2, 256, 256), BF16),
            vmem((16, 32, 256), BF16),
            vmem((TILE, 2 * KEYS), F32),
            vmem((TILE, 2 * KEYS), F32),
            pltpu.SemaphoreType.DMA((6,)),
            pltpu.SemaphoreType.DMA((128,)),
            pltpu.SemaphoreType.DMA((128,)),
            pltpu.SemaphoreType.REGULAR((3,)),
        ],
        compiler_params=pltpu.CompilerParams(
            collective_id=0, has_side_effects=True, vmem_limit_bytes=60 << 20
        ),
        name="attend_project",
    )(
        q.reshape(QROWS, 128), pk.reshape(KEYS, 128), pv.reshape(KEYS, 128),
        sk.reshape(8, 256, 128), sv.reshape(8, 256, 128), w, selfk.reshape(8, 128), selfv.reshape(8, 128), lengths,
    )


def solution(mesh):
    return jax.shard_map(
        on_device,
        mesh=mesh,
        in_specs=(
            P("seq", "tp", None),
            P("seq", "tp", None),
            P("seq", "tp", None),
            P("seq", None, "tp", None),
            P("seq", None, "tp", None),
            P("seq", "tp", None),
            P("seq", "tp", None),
            P("seq"),
            P("tp", "seq"),
        ),
        out_specs=P("tp", "seq"),
        check_vma=False,
    )
```
